128 devices in a mesh: pts: 16 (over z_lo, y, core), tau: 8 (over z_hi, x).
Axes of the slice: x: 4, y: 4, z: 4 (z_hi: 2, z_lo: 2; z = z_hi * 2 + z_lo), core: 2. Of those that a mesh axis runs over, the one named last changes fastest.
Arguments:
- occ_orbitals: bfloat16 [6144, 2048], P('pts'), may hold values from -1 to 1
- virt_orbitals: bfloat16 [6144, 4096], P('pts'), may hold values from -1 to 1
- potentials: bfloat16 [6144, 256], P('pts'), may hold values from -1 to 1
- occ_energy: float32 [2048], replicated, may hold values from -1 to -0.1
- virt_energy: float32 [4096], replicated, may hold values from 0.1 to 1
- times: float32 [8], P('tau'), may hold values from 0.25 to 4
- weights: float32 [8, 8], P(None, 'tau'), may hold values from -2 to 2
Outputs:
- screened: float32 [8, 256, 256], P('tau')
The draws below stay inside these ranges and needn't reach their ends.
All inputs are finite; a program needn't handle non-finite values.
Results may differ from the reference program's by a relative error of at most 0.0003.
Values may be sent and summed in bfloat16 or wider, within the bound.
A program may use at most 128 MiB of HBM per device.

```python
import math
import jax
import jax.numpy as jnp
from jax import lax

NOCC = 2048
NVIRT = 4096
NPOT = 256
P_DEV = 384
NP = 6144
TIMES = 8
FREQS = 8


def rough_values(key, rows, columns):
    return jax.random.normal(key, (rows, columns), jnp.float32)


def common_rows(key, columns):
    shared_key, own_key = jax.random.split(key)
    shared_part = rough_values(shared_key, P_DEV, columns)
    shared_whole = jnp.tile(shared_part, (NP // P_DEV, 1))
    own_part = rough_values(own_key, NP, columns)
    return (shared_whole, own_part)


def orbital_panel(key, columns):
    spread_key, rows_key = jax.random.split(key)
    spread = jnp.exp(jax.random.uniform(spread_key, (columns,), jnp.float32, math.log(0.5), 0.0))
    shared_whole, own_part = common_rows(rows_key, columns)
    mixed = 0.7 * shared_whole + 0.7 * own_part
    panel_values = mixed * spread / jnp.sqrt(columns * 0.541)
    return jnp.clip(panel_values, -1.0, 1.0).astype(jnp.bfloat16)


def draw_occ_orbitals(key, part):
    return orbital_panel(jax.random.fold_in(key, 11), NOCC)


def draw_virt_orbitals(key, part):
    return orbital_panel(jax.random.fold_in(key, 23), NVIRT)


def draw_potentials(key, part):
    shared_whole, own_part = common_rows(jax.random.fold_in(key, 37), NPOT)
    mixed = (0.5 * shared_whole + 0.5 * own_part) / jnp.sqrt(1.0 * P_DEV)
    return jnp.clip(mixed, -1.0, 1.0).astype(jnp.bfloat16)


def block_scale(rng, extent, cuts, smallest, largest):
    factor_of = 1.0
    for axis_at, parts in cuts:
        heights = jax.random.uniform(jax.random.fold_in(jax.random.fold_in(rng, 6), axis_at), (parts,), jnp.float32, smallest / len(cuts), largest / len(cuts))
        factor_of = factor_of * jnp.repeat(jnp.exp(heights), extent[axis_at] // parts).reshape((-1,) + (1,) * (len(extent) - 1 - axis_at))
    return factor_of


def noise(key, extent, scale, bound, shards=(), held_as=jnp.bfloat16):
    entries = jax.random.normal(key, extent, jnp.float32) * scale
    if len(shards) > 0:
        entries = block_scale(key, extent, shards, -0.22, 0.18) * entries
    return jnp.clip(entries, min=-bound, max=bound).astype(held_as)


def setup_inputs(seed: int = 0) -> dict:
    key_of = jax.random.split(jax.random.key(seed), 8)
    occ_orbitals = draw_occ_orbitals(jax.random.fold_in(key_of[7], 71), 0)
    virt_orbitals = draw_virt_orbitals(jax.random.fold_in(key_of[7], 71), 0)
    potentials = draw_potentials(jax.random.fold_in(key_of[7], 71), 0)
    occ_energy = jnp.clip(jax.random.uniform(key_of[3], (NOCC,), jnp.float32, -1.0, -0.1), -1.0, -0.1)
    virt_energy = jnp.clip(jax.random.uniform(key_of[4], (NVIRT,), jnp.float32, 0.1, 1.0), 0.1, 1.0)
    times = jnp.clip(jnp.exp(math.log(4.0) - 2.7725887 * jax.random.uniform(key_of[5], (TIMES,), jnp.float32) ** block_scale(key_of[5], (TIMES,), ((0, 8),), -0.2, 0.2)), 0.25, 4.0)
    weights = noise(key_of[6], (FREQS, TIMES), TIMES ** -0.5, 2.0, ((1, 8),), jnp.float32)
    return {"occ_orbitals": occ_orbitals, "virt_orbitals": virt_orbitals, "potentials": potentials, "occ_energy": occ_energy, "virt_energy": virt_energy, "times": times, "weights": weights}


def reference(occ_orbitals, virt_orbitals, potentials, occ_energy, virt_energy, times, weights):
    pot_wide = potentials.astype(jnp.float32)
    contract = (((1,), (1,)), ((), ()))

    def one_time(moment):
        occ_half = (occ_orbitals.astype(jnp.float32) * jnp.exp(0.5 * moment * occ_energy)).astype(jnp.bfloat16)
        virt_half = (virt_orbitals.astype(jnp.float32) * jnp.exp(-0.5 * moment * virt_energy)).astype(jnp.bfloat16)
        green_occ = lax.dot_general(occ_half, occ_half, contract, preferred_element_type=jnp.float32)
        green_virt = lax.dot_general(virt_half, virt_half, contract, preferred_element_type=jnp.float32)
        response = (-(green_occ * green_virt)).astype(jnp.bfloat16)
        applied = jnp.dot(response, potentials, preferred_element_type=jnp.float32)
        return lax.dot_general(pot_wide, applied, (((0,), (0,)), ((), ())), precision=lax.Precision.HIGHEST)

    projected = lax.map(one_time, times)
    return jnp.einsum("wt,tab->wab", weights.astype(jnp.float32), projected, precision=lax.Precision.HIGHEST)
```

```python
import functools

import jax
import jax.numpy as jnp
from jax import lax
from jax.experimental import pallas as pl
from jax.experimental.pallas import tpu as pltpu
from jax.sharding import PartitionSpec as P

MESH = pl.DeviceIdType.MESH
NT = (((1,), (1,)), ((), ()))
N_OCC, N_VIRT, N_POT, ROWS = 2048, 4096, 256, 384
N_ORB = N_OCC + N_VIRT
WIDTH = N_ORB + N_POT
TIMES = 8
SLAB = ROWS // TIMES
CHUNK = 16
CHUNKS = SLAB // CHUNK
OWN, A, B, C, D = range(5)
F32, BF16 = jnp.float32, jnp.bfloat16


def kernel(
    occ_ref, virt_ref, pot_ref, energy_ref, tw_ref, out_ref,
    own, far, relay, scaled, resp, applied, factor, tw_all, pot_far, proj,
    load_sem, send_sem, recv_sem, tw_send, tw_recv,
):
    pts, tau = lax.axis_index("pts"), lax.axis_index("tau")
    z_lo, y, core = pts // 8, (pts // 2) % 4, pts % 2
    z_hi, x = tau // 4, tau % 4

    def at(z_lo_=None, y_=None, core_=None, z_hi_=None):
        zl = z_lo if z_lo_ is None else z_lo_
        yy = y if y_ is None else y_
        cc = core if core_ is None else core_
        zh = z_hi if z_hi_ is None else z_hi_
        return (zl * 8 + yy * 2 + cc, zh * 4 + x)

    sibling = at(core_=1 - core)
    z_out = at(z_lo_=1 - z_lo, z_hi_=1 - z_hi)
    z_in = at(z_lo_=1 - z_lo)
    y_down = at(y_=(y + 3) % 4)
    y_up = at(y_=(y + 1) % 4)
    tau_peers = [(pts, (tau + d) % TIMES) for d in range(1, TIMES)]

    first = pl.multiple_of(tau * SLAB, CHUNK)
    parts = ((occ_ref, 0, N_OCC), (virt_ref, N_OCC, N_VIRT), (pot_ref, N_ORB, N_POT))
    loads = []
    for i, (ref, at_col, cols) in enumerate(parts):
        loads.append(pltpu.make_async_copy(
            ref.at[pl.ds(first, SLAB)], far.at[OWN, :, pl.ds(at_col, cols)], load_sem.at[i]))
    for i, (ref, at_col, cols) in enumerate(parts):
        loads.append(pltpu.make_async_copy(
            ref, own.at[pl.ds(0, ROWS), pl.ds(at_col, cols)], load_sem.at[3 + i]))
    for load in loads:
        load.start()

    barrier = pltpu.get_barrier_semaphore()
    greeted = [sibling, z_out, z_in, y_down, y_up] + tau_peers
    for peer in greeted:
        pl.semaphore_signal(barrier, 1, device_id=peer, device_id_type=MESH)
    tw_all[tau] = tw_ref[...]
    pl.semaphore_wait(barrier, len(greeted))

    count = iter(range(64))
    sent = []

    def send(src, dst, peer):
        i = next(count)
        copy = pltpu.make_async_remote_copy(
            src_ref=src, dst_ref=dst, send_sem=send_sem.at[i], recv_sem=recv_sem.at[i],
            device_id=peer, device_id_type=MESH)
        copy.start()
        sent.append(copy)
        return copy

    tw_copies = []
    for i, peer in enumerate(tau_peers):
        copy = pltpu.make_async_remote_copy(
            src_ref=tw_ref, dst_ref=tw_all.at[tau], send_sem=tw_send.at[i], recv_sem=tw_recv.at[i],
            device_id=peer, device_id_type=MESH)
        copy.start()
        tw_copies.append(copy)

    def rows_of(k):
        return pl.ds(k * CHUNK, CHUNK)

    for load in loads[:3]:
        load.wait()
    got_b = [send(far.at[OWN, rows_of(k)], far.at[B, rows_of(k)], y_down) for k in range(CHUNKS)]
    for load in loads[3:]:
        load.wait()
    out_first = ((1 - z_hi) * 4 + x) * SLAB
    got_a = {}
    for k in (1, 2, 0):
        rows = pl.ds(pl.multiple_of(out_first + k * CHUNK, CHUNK), CHUNK)
        got_a[k] = send(own.at[rows], far.at[A, rows_of(k)], z_out)
    got_own = send(own.at[pl.ds(0, ROWS)], own.at[pl.ds(ROWS, ROWS)], sibling)

    for copy in tw_copies:
        copy.wait()
    for t in range(TIMES):
        factor[t] = jnp.exp(tw_all[t, 8:9, 0:1] * energy_ref[...])

    def scale(slot, k, t_first, t_count):
        def one(i, carry):
            t = t_first + i
            wide = far[slot, rows_of(k), pl.ds(0, N_ORB)].astype(F32) * factor[t]
            scaled[pl.ds(pl.multiple_of(i * SLAB + k * CHUNK, CHUNK), CHUNK)] = wide.astype(BF16)
            return carry
        lax.fori_loop(0, t_count, one, 0)

    def tile(n, t_count):
        lines = t_count * SLAB
        n0 = pl.multiple_of(n * 256, 256)
        g_occ = lax.dot_general(
            scaled[:lines, :N_OCC], own[pl.ds(n0, 256), :N_OCC], NT, preferred_element_type=F32)
        g_virt = lax.dot_general(
            scaled[:lines, N_OCC:], own[pl.ds(n0, 256), N_OCC:N_ORB], NT, preferred_element_type=F32)
        resp[:lines, pl.ds(n0, 256)] = (-(g_occ * g_virt)).astype(BF16)

    def apply(slot, t_first, t_count):
        lines = t_count * SLAB
        part = jnp.dot(resp[:lines], own[:, N_ORB:], preferred_element_type=F32)
        applied[pl.ds(t_first, t_count), slot * SLAB:(slot + 1) * SLAB, :] = part.reshape(
            t_count, SLAB, N_POT)

    for k in range(CHUNKS):
        scale(OWN, k, 0, TIMES)
    tile(0, TIMES)
    got_own.wait_recv()
    tile(1, TIMES)
    got_c, got_relay, got_d = [], {}, {}

    def pass_c(k):
        got_b[k].wait_recv()
        got_c.append(send(far.at[B, rows_of(k)], far.at[C, rows_of(k)], z_in))

    def pass_up(k):
        got_a[k].wait_recv()
        slot = jnp.where((y + 2) % 4 < 2, OWN, A)
        got_relay[k] = send(far.at[slot, rows_of(k)], relay.at[k - 1], y_up)

    def pass_d(k):
        got_relay[k].wait_recv()
        got_d[k] = send(relay.at[k - 1], far.at[D, rows_of(k)], y_up)

    pass_c(0)
    pass_up(1)
    tile(2, TIMES)
    apply(OWN, 0, TIMES)
    pass_c(1)
    pass_up(2)
    half = TIMES // 2
    t_mine, t_other = z_lo * half, (1 - z_lo) * half
    scale(A, 1, t_mine, half)
    scale(A, 2, t_mine, half)
    got_a[0].wait_recv()
    scale(A, 0, t_mine, half)
    for n in range(3):
        tile(n, half)
    apply(A, t_mine, half)
    applied[pl.ds(t_other, half), A * SLAB:(A + 1) * SLAB, :] = jnp.zeros((half, SLAB, N_POT), F32)
    pass_c(2)
    pass_d(1)
    got_c[0].wait_recv()
    slot = jnp.where((y + 3) % 4 < 2, B, C)
    got_d[0] = send(far.at[slot, rows_of(0)], far.at[D, rows_of(0)], y_down)
    for k in range(CHUNKS):
        scale(B, k, 0, TIMES)
    tile(0, TIMES)
    pass_d(2)
    tile(1, TIMES)
    tile(2, TIMES)
    apply(B, 0, TIMES)
    for k in range(CHUNKS):
        if k:
            got_c[k].wait_recv()
        scale(C, k, 0, TIMES)
    for n in range(3):
        tile(n, TIMES)
    apply(C, 0, TIMES)
    for k in range(CHUNKS):
        got_d[k].wait_recv()
        scale(D, k, 0, TIMES)
    for n in range(3):
        tile(n, TIMES)
    apply(D, 0, TIMES)

    pot_far[0:SLAB] = far[OWN, :, N_ORB:] * jnp.asarray(0.5, BF16)
    for slot in (A, B, C, D):
        pot_far[slot * SLAB:(slot + 1) * SLAB] = far[slot, :, N_ORB:]
    used = 5 * SLAB
    pot_far[used:] = jnp.zeros((N_POT - used, N_POT), BF16)
    pot_t = pot_far[...].T
    applied[:, used:, :] = jnp.zeros((TIMES, N_POT - used, N_POT), F32)

    def project(t, carry):
        whole = applied[t]
        high = whole.astype(BF16)
        low = (whole - high.astype(F32)).astype(BF16)
        both = jnp.dot(pot_t, high, preferred_element_type=F32) + jnp.dot(
            pot_t, low, preferred_element_type=F32)
        proj[t, 0:128] = both[:128, :128]
        proj[t, 128:256] = both[:128, 128:] + both[128:, :128].T
        proj[t, 256:384] = both[128:, 128:]
        return carry

    lax.fori_loop(0, TIMES, project, 0)

    def combine(w, carry):
        total = tw_all[0, pl.ds(w, 1), :] * proj[0]
        for t in range(1, TIMES):
            total = total + tw_all[t, pl.ds(w, 1), :] * proj[t]
        out_ref[w] = total
        return carry

    lax.fori_loop(0, TIMES, combine, 0)
    for copy in sent:
        copy.wait_send()


def body(occ, virt, pot, occ_energy, virt_energy, times, weights):
    energy = jnp.concatenate([occ_energy, -virt_energy])[None, :]
    tw = jnp.concatenate(
        [jnp.broadcast_to(weights, (TIMES, 128)), jnp.broadcast_to(times[None, :], (8, 128))], axis=0)
    anywhere, vmem = pl.BlockSpec(memory_space=pl.ANY), pl.BlockSpec(memory_space=pltpu.VMEM)
    sums = pl.pallas_call(
        kernel,
        out_shape=jax.ShapeDtypeStruct((TIMES, 384, 128), F32),
        in_specs=[anywhere] * 3 + [vmem] * 2,
        out_specs=vmem,
        scratch_shapes=[
            pltpu.VMEM((2 * ROWS, WIDTH), BF16),
            pltpu.VMEM((5, SLAB, WIDTH), BF16),
            pltpu.VMEM((2, CHUNK, WIDTH), BF16),
            pltpu.VMEM((TIMES * SLAB, N_ORB), BF16),
            pltpu.VMEM((TIMES * SLAB, 2 * ROWS), BF16),
            pltpu.VMEM((TIMES, N_POT, N_POT), F32),
            pltpu.VMEM((TIMES, 1, N_ORB), F32),
            pltpu.VMEM((TIMES, 16, 128), F32),
            pltpu.VMEM((N_POT, N_POT), BF16),
            pltpu.VMEM((TIMES, 384, 128), F32),
            pltpu.SemaphoreType.DMA((6,)),
            pltpu.SemaphoreType.DMA((24,)),
            pltpu.SemaphoreType.DMA((24,)),
            pltpu.SemaphoreType.DMA((7,)),
            pltpu.SemaphoreType.DMA((7,)),
        ],
        compiler_params=pltpu.CompilerParams(
            collective_id=0, has_side_effects=True, vmem_limit_bytes=48 * 2**20),
    )(occ, virt, pot, energy, tw)
    mine = lax.psum_scatter(sums, "tau", scatter_dimension=0, tiled=True)
    mine = lax.psum(mine, "pts")[0]
    low, mid, high = mine[:128], mine[128:256], mine[256:]
    top = jnp.concatenate([low + low.T, mid], axis=1)
    bottom = jnp.concatenate([mid.T, high + high.T], axis=1)
    return jnp.concatenate([top, bottom], axis=0)[None]


def solution(mesh):
    return jax.shard_map(
        body,
        mesh=mesh,
        in_specs=(P("pts", None), P("pts", None), P("pts", None), P(), P(), P("tau"), P(None, "tau")),
        out_specs=P("tau", None, None),
        check_vma=False,
    )
```

```python
import functools

import jax
import jax.numpy as jnp
from jax import lax
from jax.experimental import pallas as pl
from jax.experimental.pallas import tpu as pltpu
from jax.sharding import PartitionSpec as P

MESH = pl.DeviceIdType.MESH
NT = (((1,), (1,)), ((), ()))
N_OCC, N_VIRT, N_POT, ROWS = 2048, 4096, 256, 384
N_ORB = N_OCC + N_VIRT
WIDTH = N_ORB + N_POT
TIMES = 8
SLAB = ROWS // TIMES
CHUNK = 16
CHUNKS = SLAB // CHUNK
OWN, A, B, C, D = range(5)
F32, BF16 = jnp.float32, jnp.bfloat16


def kernel(
    occ_ref, virt_ref, pot_ref, occ_e_ref, virt_e_ref, times_ref, weights_ref, out_ref,
    own, far, relay, scaled, resp, applied, factor, tw_mine, tw_all, pot_far, proj,
    sums, from_core, arrive1, arrive2, arrive3, left1, left2, final, whole_out,
    load_sem, send_sem, recv_sem, tw_send, tw_recv,
    core_sem, ring_send, ring_recv, all_send, all_recv,
):
    pts, tau = lax.axis_index("pts"), lax.axis_index("tau")
    z_lo, y, core = pts // 8, (pts // 2) % 4, pts % 2
    z_hi, x = tau // 4, tau % 4

    def at(z_lo_=None, y_=None, core_=None, z_hi_=None):
        zl = z_lo if z_lo_ is None else z_lo_
        yy = y if y_ is None else y_
        cc = core if core_ is None else core_
        zh = z_hi if z_hi_ is None else z_hi_
        return (zl * 8 + yy * 2 + cc, zh * 4 + x)

    sibling = at(core_=1 - core)
    z_out = at(z_lo_=1 - z_lo, z_hi_=1 - z_hi)
    z_in = at(z_lo_=1 - z_lo)
    y_down = at(y_=(y + 3) % 4)
    y_up = at(y_=(y + 1) % 4)
    tau_peers = [(pts, (tau + d) % TIMES) for d in range(1, TIMES)]

    first = pl.multiple_of(tau * SLAB, CHUNK)
    parts = ((occ_ref, 0, N_OCC), (virt_ref, N_OCC, N_VIRT), (pot_ref, N_ORB, N_POT))
    loads = []
    for i, (ref, at_col, cols) in enumerate(parts):
        loads.append(pltpu.make_async_copy(
            ref.at[pl.ds(first, SLAB)], far.at[OWN, :, pl.ds(at_col, cols)], load_sem.at[i]))
    for i, (ref, at_col, cols) in enumerate(parts):
        loads.append(pltpu.make_async_copy(
            ref, own.at[pl.ds(0, ROWS), pl.ds(at_col, cols)], load_sem.at[3 + i]))
    for load in loads:
        load.start()

    barrier = pltpu.get_barrier_semaphore()
    pts_peers = [((pts + d) % 16, tau) for d in range(1, 16)]
    greeted = [z_out] + pts_peers + tau_peers
    for peer in greeted:
        pl.semaphore_signal(barrier, 1, device_id=peer, device_id_type=MESH)
    tw_mine[0:8] = jnp.broadcast_to(weights_ref[...], (8, 128))
    tw_mine[8:16] = jnp.broadcast_to(times_ref[...], (8, 128))
    tw_all[tau] = tw_mine[...]
    pl.semaphore_wait(barrier, len(greeted))

    count = iter(range(64))
    sent = []

    def send(src, dst, peer):
        i = next(count)
        copy = pltpu.make_async_remote_copy(
            src_ref=src, dst_ref=dst, send_sem=send_sem.at[i], recv_sem=recv_sem.at[i],
            device_id=peer, device_id_type=MESH)
        copy.start()
        sent.append(copy)
        return copy

    tw_copies = []
    for i, peer in enumerate(tau_peers):
        copy = pltpu.make_async_remote_copy(
            src_ref=tw_mine, dst_ref=tw_all.at[tau], send_sem=tw_send.at[i], recv_sem=tw_recv.at[i],
            device_id=peer, device_id_type=MESH)
        copy.start()
        tw_copies.append(copy)

    def rows_of(k):
        return pl.ds(k * CHUNK, CHUNK)

    for load in loads[:3]:
        load.wait()
    got_b = [send(far.at[OWN, rows_of(k)], far.at[B, rows_of(k)], y_down) for k in range(CHUNKS)]
    for load in loads[3:]:
        load.wait()
    out_first = ((1 - z_hi) * 4 + x) * SLAB
    got_a = {}
    for k in (1, 2, 0):
        rows = pl.ds(pl.multiple_of(out_first + k * CHUNK, CHUNK), CHUNK)
        got_a[k] = send(own.at[rows], far.at[A, rows_of(k)], z_out)
    got_own = send(own.at[pl.ds(0, ROWS)], own.at[pl.ds(ROWS, ROWS)], sibling)

    for copy in tw_copies:
        copy.wait_recv()
    for t in range(TIMES):
        moment = tw_all[t, 8:9, 0:1]
        factor[t, :, :N_OCC] = jnp.exp(moment * occ_e_ref[...])
        factor[t, :, N_OCC:] = jnp.exp(-moment * virt_e_ref[...])

    def scale(slot, k, t_first, t_count):
        def one(i, carry):
            t = t_first + i
            wide = far[slot, rows_of(k), pl.ds(0, N_ORB)].astype(F32) * factor[t]
            scaled[pl.ds(pl.multiple_of(i * SLAB + k * CHUNK, CHUNK), CHUNK)] = wide.astype(BF16)
            return carry
        lax.fori_loop(0, t_count, one, 0)

    def tile(n, t_count):
        lines = t_count * SLAB
        n0 = pl.multiple_of(n * 256, 256)
        g_occ = lax.dot_general(
            scaled[:lines, :N_OCC], own[pl.ds(n0, 256), :N_OCC], NT, preferred_element_type=F32)
        g_virt = lax.dot_general(
            scaled[:lines, N_OCC:], own[pl.ds(n0, 256), N_OCC:N_ORB], NT, preferred_element_type=F32)
        resp[:lines, pl.ds(n0, 256)] = (-(g_occ * g_virt)).astype(BF16)

    def apply(slot, t_first, t_count):
        lines = t_count * SLAB
        part = jnp.dot(resp[:lines], own[:, N_ORB:], preferred_element_type=F32)
        applied[pl.ds(t_first, t_count), slot * SLAB:(slot + 1) * SLAB, :] = part.reshape(
            t_count, SLAB, N_POT)

    for k in range(CHUNKS):
        scale(OWN, k, 0, TIMES)
    tile(0, TIMES)
    got_own.wait_recv()
    tile(1, TIMES)
    got_c, got_relay, got_d = [], {}, {}

    def pass_c(k):
        got_b[k].wait_recv()
        got_c.append(send(far.at[B, rows_of(k)], far.at[C, rows_of(k)], z_in))

    def pass_up(k):
        got_a[k].wait_recv()
        slot = jnp.where((y + 2) % 4 < 2, OWN, A)
        got_relay[k] = send(far.at[slot, rows_of(k)], relay.at[k - 1], y_up)

    def pass_d(k):
        got_relay[k].wait_recv()
        got_d[k] = send(relay.at[k - 1], far.at[D, rows_of(k)], y_up)

    pass_c(0)
    pass_up(1)
    tile(2, TIMES)
    apply(OWN, 0, TIMES)
    pass_c(1)
    pass_up(2)
    half = TIMES // 2
    t_mine, t_other = z_lo * half, (1 - z_lo) * half
    scale(A, 1, t_mine, half)
    scale(A, 2, t_mine, half)
    got_a[0].wait_recv()
    scale(A, 0, t_mine, half)
    for n in range(3):
        tile(n, half)
    apply(A, t_mine, half)
    applied[pl.ds(t_other, half), A * SLAB:(A + 1) * SLAB, :] = jnp.zeros((half, SLAB, N_POT), F32)
    pass_c(2)
    pass_d(1)
    got_c[0].wait_recv()
    slot = jnp.where((y + 3) % 4 < 2, B, C)
    got_d[0] = send(far.at[slot, rows_of(0)], far.at[D, rows_of(0)], y_down)
    for k in range(CHUNKS):
        scale(B, k, 0, TIMES)
    tile(0, TIMES)
    pass_d(2)
    tile(1, TIMES)
    tile(2, TIMES)
    apply(B, 0, TIMES)
    for k in range(CHUNKS):
        if k:
            got_c[k].wait_recv()
        scale(C, k, 0, TIMES)
    for n in range(3):
        tile(n, TIMES)
    apply(C, 0, TIMES)
    for k in range(CHUNKS):
        got_d[k].wait_recv()
        scale(D, k, 0, TIMES)
    for n in range(3):
        tile(n, TIMES)
    apply(D, 0, TIMES)

    pot_far[0:SLAB] = far[OWN, :, N_ORB:] * jnp.asarray(0.5, BF16)
    for slot in (A, B, C, D):
        pot_far[slot * SLAB:(slot + 1) * SLAB] = far[slot, :, N_ORB:]
    used = 5 * SLAB
    pot_far[used:] = jnp.zeros((N_POT - used, N_POT), BF16)
    pot_t = pot_far[...].T
    applied[:, used:, :] = jnp.zeros((TIMES, N_POT - used, N_POT), F32)

    def project(t, carry):
        whole = applied[t]
        high = whole.astype(BF16)
        low = (whole - high.astype(F32)).astype(BF16)
        both = jnp.dot(pot_t, high, preferred_element_type=F32) + jnp.dot(
            pot_t, low, preferred_element_type=F32)
        proj[t, 0:128] = both[:128, :128]
        proj[t, 128:256] = both[:128, 128:] + both[128:, :128].T
        proj[t, 256:384] = both[128:, 128:]
        return carry

    lax.fori_loop(0, TIMES, project, 0)

    def combine(w, carry):
        w_zh, w_x = w // 4, w % 4
        weight = [tw_all[t, pl.ds(w, 1), :] for t in range(TIMES)]
        for h in range(2):
            for a in range(3):
                for zl in range(2):
                    for yy in range(4):
                        rows = pl.ds(((h * 3 + a) * 8 + zl * 4 + yy) * 8, 8)
                        total = weight[0] * proj[0, rows]
                        for t in range(1, TIMES):
                            total = total + weight[t] * proj[t, rows]
                        zz = w_zh * 2 + zl
                        place = ((w_x, yy, zz), (yy, zz, w_x), (zz, w_x, yy))[a]
                        sums[h, a, place[0], place[1], place[2]] = total
        return carry

    lax.fori_loop(0, TIMES, combine, 0)

    swap = pltpu.make_async_remote_copy(
        src_ref=sums.at[1 - core], dst_ref=from_core, send_sem=core_sem.at[0], recv_sem=core_sem.at[1],
        device_id=sibling, device_id_type=MESH)
    swap.start()
    swap.wait_recv()
    z = z_hi * 2 + z_lo
    place = (x, y, z)

    def along(axis, index):
        if axis == 0:
            return (pts, z_hi * 4 + index)
        if axis == 1:
            return at(y_=index)
        return at(z_lo_=index % 2, z_hi_=index // 2)

    for a in range(3):
        from_core[a] = from_core[a] + sums[core, a]
    held = from_core
    copies = []
    for stage, (arrive, left) in enumerate(((arrive1, left1), (arrive2, left2), (arrive3, final))):
        wave = []
        for a in range(3):
            axis = (a + stage) % 3
            for d in (2, 1, 3):
                index = (place[axis] + d) % 4
                i = (stage * 3 + a) * 3 + d - 1
                copy = pltpu.make_async_remote_copy(
                    src_ref=held.at[a, index], dst_ref=arrive.at[a, d - 1],
                    send_sem=ring_send.at[i], recv_sem=ring_recv.at[i],
                    device_id=along(axis, index), device_id_type=MESH)
                copy.start()
                wave.append(copy)
        copies += wave
        for a in range(3):
            for copy in wave[3 * a:3 * a + 3]:
                copy.wait_recv()
            left[a] = held[a, place[(a + stage) % 3]] + arrive[a, 0] + arrive[a, 1] + arrive[a, 2]
        held = left

    wave = []
    for i, peer in enumerate(pts_peers):
        copy = pltpu.make_async_remote_copy(
            src_ref=final, dst_ref=whole_out.at[pts], send_sem=all_send.at[i], recv_sem=all_recv.at[i],
            device_id=peer, device_id_type=MESH)
        copy.start()
        wave.append(copy)
    whole_out[pts] = final[...]
    for copy in wave:
        copy.wait_recv()
    rows = []
    for h in range(2):
        for a in range(3):
            for zl in range(2):
                for yy in range(4):
                    rows.append(whole_out[zl * 8 + yy * 2 + h, a])
    low, mid, high = [jnp.concatenate(rows[16 * b:16 * b + 16], axis=0) for b in range(3)]
    out_ref[0, :128, :128] = low + low.T
    out_ref[0, :128, 128:] = mid
    out_ref[0, 128:, :128] = mid.T
    out_ref[0, 128:, 128:] = high + high.T
    swap.wait_send()
    for copy in sent + copies + wave + tw_copies:
        copy.wait_send()


def body(occ, virt, pot, occ_energy, virt_energy, times, weights):
    anywhere, vmem = pl.BlockSpec(memory_space=pl.ANY), pl.BlockSpec(memory_space=pltpu.VMEM)
    return pl.pallas_call(
        kernel,
        out_shape=jax.ShapeDtypeStruct((1, N_POT, N_POT), F32),
        in_specs=[anywhere] * 3 + [vmem] * 4,
        out_specs=vmem,
        scratch_shapes=[
            pltpu.VMEM((2 * ROWS, WIDTH), BF16),
            pltpu.VMEM((5, SLAB, WIDTH), BF16),
            pltpu.VMEM((2, CHUNK, WIDTH), BF16),
            pltpu.VMEM((TIMES * SLAB, N_ORB), BF16),
            pltpu.VMEM((TIMES * SLAB, 2 * ROWS), BF16),
            pltpu.VMEM((TIMES, N_POT, N_POT), F32),
            pltpu.VMEM((TIMES, 1, N_ORB), F32),
            pltpu.VMEM((16, 128), F32),
            pltpu.VMEM((TIMES, 16, 128), F32),
            pltpu.VMEM((N_POT, N_POT), BF16),
            pltpu.VMEM((TIMES, 384, 128), F32),
            pltpu.VMEM((2, 3, 4, 4, 4, 8, 128), F32),
            pltpu.VMEM((3, 4, 4, 4, 8, 128), F32),
            pltpu.VMEM((3, 3, 4, 4, 8, 128), F32),
            pltpu.VMEM((3, 3, 4, 8, 128), F32),
            pltpu.VMEM((3, 3, 8, 128), F32),
            pltpu.VMEM((3, 4, 4, 8, 128), F32),
            pltpu.VMEM((3, 4, 8, 128), F32),
            pltpu.VMEM((3, 8, 128), F32),
            pltpu.VMEM((16, 3, 8, 128), F32),
            pltpu.SemaphoreType.DMA((6,)),
            pltpu.SemaphoreType.DMA((24,)),
            pltpu.SemaphoreType.DMA((24,)),
            pltpu.SemaphoreType.DMA((7,)),
            pltpu.SemaphoreType.DMA((7,)),
            pltpu.SemaphoreType.DMA((2,)),
            pltpu.SemaphoreType.DMA((27,)),
            pltpu.SemaphoreType.DMA((27,)),
            pltpu.SemaphoreType.DMA((15,)),
            pltpu.SemaphoreType.DMA((15,)),
        ],
        compiler_params=pltpu.CompilerParams(
            collective_id=0, has_side_effects=True, vmem_limit_bytes=60 * 2**20),
    )(occ, virt, pot, occ_energy[None, :], virt_energy[None, :], times[None, :], weights)


def solution(mesh):
    return jax.shard_map(
        body,
        mesh=mesh,
        in_specs=(P("pts", None), P("pts", None), P("pts", None), P(), P(), P("tau"), P(None, "tau")),
        out_specs=P("tau", None, None),
        check_vma=False,
    )
```

```python
import functools

import jax
import jax.numpy as jnp
from jax import lax
from jax.experimental import pallas as pl
from jax.experimental.pallas import tpu as pltpu
from jax.sharding import PartitionSpec as P

MESH = pl.DeviceIdType.MESH
NT = (((1,), (1,)), ((), ()))
N_OCC, N_VIRT, N_POT, ROWS = 2048, 4096, 256, 384
N_ORB = N_OCC + N_VIRT
WIDTH = N_ORB + N_POT
TIMES = 8
SLAB = ROWS // TIMES
CHUNK = 16
CHUNKS = SLAB // CHUNK
OWN, B, C, D, A = range(5)
F32, BF16 = jnp.float32, jnp.bfloat16


def kernel(
    occ_ref, virt_ref, pot_ref, occ_e_ref, virt_e_ref, times_ref, weights_ref, out_ref,
    own, far, relay, scaled, resp, applied, factor, tw_all, pot_far, proj,
    sums, from_core, arrive1, arrive2, arrive3, left1, left2, final, quad, whole_out,
    load_sem, send_sem, recv_sem, tw_send, tw_recv,
    core_sem, ring_send, ring_recv, all_send, all_recv,
):
    pts, tau = lax.axis_index("pts"), lax.axis_index("tau")
    z_lo, y, core = pts // 8, (pts // 2) % 4, pts % 2
    z_hi, x = tau // 4, tau % 4

    def at(z_lo_=None, y_=None, core_=None, z_hi_=None):
        zl = z_lo if z_lo_ is None else z_lo_
        yy = y if y_ is None else y_
        cc = core if core_ is None else core_
        zh = z_hi if z_hi_ is None else z_hi_
        return (zl * 8 + yy * 2 + cc, zh * 4 + x)

    sibling = at(core_=1 - core)
    z_out = at(z_lo_=1 - z_lo, z_hi_=1 - z_hi)
    z_in = at(z_lo_=1 - z_lo)
    y_down = at(y_=(y + 3) % 4)
    y_up = at(y_=(y + 1) % 4)
    z_in_sibling = at(z_lo_=1 - z_lo, core_=1 - core)
    z_far = at(z_hi_=1 - z_hi)
    x_peers = [(pts, z_hi * 4 + (x + d) % 4) for d in range(1, 4)]
    y_across = at(y_=(y + 2) % 4)

    first = pl.multiple_of(tau * SLAB, CHUNK)
    parts = ((occ_ref, 0, N_OCC), (virt_ref, N_OCC, N_VIRT), (pot_ref, N_ORB, N_POT))
    loads = []
    for i, (ref, at_col, cols) in enumerate(parts):
        loads.append(pltpu.make_async_copy(
            ref.at[pl.ds(first, SLAB)], far.at[OWN, :, pl.ds(at_col, cols)], load_sem.at[i]))
    for i, (ref, at_col, cols) in enumerate(parts):
        loads.append(pltpu.make_async_copy(
            ref, own.at[pl.ds(0, ROWS), pl.ds(at_col, cols)], load_sem.at[3 + i]))
    for load in loads:
        load.start()

    barrier = pltpu.get_barrier_semaphore()
    greeted = [sibling, z_in, z_in_sibling, z_out, z_far, y_down, y_up, y_across] + x_peers
    for peer in greeted:
        pl.semaphore_signal(barrier, 1, device_id=peer, device_id_type=MESH)
    here = x * 2 + z_hi
    for w in range(TIMES):
        tw_all[here, w:w + 1] = jnp.full((1, 128), weights_ref[0, w], F32)
    tw_all[here, 8:16] = jnp.full((8, 128), times_ref[0], F32)
    pl.semaphore_wait(barrier, len(greeted))

    count = iter(range(64))
    sent = []

    def to(src, dst, peer):
        i = next(count)
        copy = pltpu.make_async_remote_copy(
            src_ref=src, dst_ref=dst, send_sem=send_sem.at[i], recv_sem=recv_sem.at[i],
            device_id=peer, device_id_type=MESH)
        sent.append(copy)
        return copy

    def send(src, dst, peer):
        copy = to(src, dst, peer)
        copy.start()
        return copy

    def send_tw(i, first, tiles, peer):
        copy = pltpu.make_async_remote_copy(
            src_ref=tw_all.at[pl.ds(first, tiles)], dst_ref=tw_all.at[pl.ds(first, tiles)],
            send_sem=tw_send.at[i], recv_sem=tw_recv.at[i], device_id=peer, device_id_type=MESH)
        copy.start()
        return copy

    tw_copies = [send_tw(0, here, 1, z_far)]

    def rows_of(k):
        return pl.ds(k * CHUNK, CHUNK)

    for load in loads[:3]:
        load.wait()
    got_b = [send(far.at[OWN, rows_of(k)], far.at[B, rows_of(k)], y_down) for k in range(CHUNKS)]
    for load in loads[3:]:
        load.wait()
    out_first = ((1 - z_hi) * 4 + x) * SLAB

    def own_rows(start, k):
        return own.at[pl.ds(pl.multiple_of(start + k * CHUNK, CHUNK), CHUNK)]

    got_a = {
        2: send(own_rows(first, 2), far.at[A, rows_of(2)], z_in),
        1: send(own_rows(out_first, 1), far.at[A, rows_of(1)], z_out),
        0: send(own_rows(out_first, 0), far.at[A, rows_of(0)], z_out),
    }
    got_own = send(own.at[pl.ds(0, ROWS)], own.at[pl.ds(ROWS, ROWS)], sibling)

    tw_copies[0].wait_recv()
    tw_copies += [send_tw(1 + i, x * 2, 2, peer) for i, peer in enumerate(x_peers)]
    for copy in tw_copies[1:]:
        copy.wait_recv()

    def tw_at(t):
        return (t % 4) * 2 + t // 4

    for t in range(TIMES):
        moment = tw_all[tw_at(t), 8:9, 0:1]
        factor[t, :, :N_OCC] = jnp.exp(moment * occ_e_ref[...])
        factor[t, :, N_OCC:] = jnp.exp(-moment * virt_e_ref[...])

    def scale(slot, t_first, t_count):
        def one(i, carry):
            rows = pl.ds(pl.multiple_of((i % CHUNKS) * CHUNK, CHUNK), CHUNK)
            wide = far[slot, rows, pl.ds(0, N_ORB)].astype(F32) * factor[t_first + i // CHUNKS]
            scaled[pl.ds(pl.multiple_of(i * CHUNK, CHUNK), CHUNK)] = wide.astype(BF16)
            return carry
        lax.fori_loop(0, t_count * CHUNKS, one, 0)

    def tile(n, t_count):
        lines = t_count * SLAB
        n0 = pl.multiple_of(n * 256, 256)
        g_occ = lax.dot_general(
            scaled[:lines, :N_OCC], own[pl.ds(n0, 256), :N_OCC], NT, preferred_element_type=F32)
        g_virt = lax.dot_general(
            scaled[:lines, N_OCC:], own[pl.ds(n0, 256), N_OCC:N_ORB], NT, preferred_element_type=F32)
        resp[:lines, pl.ds(n0, 256)] = (-(g_occ * g_virt)).astype(BF16)

    def apply(slot, t_first, t_count):
        lines = t_count * SLAB
        part = jnp.dot(resp[:lines], own[:, N_ORB:], preferred_element_type=F32)
        rows = pl.ds(pl.multiple_of(slot * SLAB, CHUNK), SLAB)
        applied[pl.ds(t_first, t_count), rows, :] = part.reshape(t_count, SLAB, N_POT)

    got_c = [to(far.at[B, rows_of(k)], far.at[C, rows_of(k)], z_in) for k in range(CHUNKS)]
    up_slot = jnp.where((y + 2) % 4 < 2, OWN, A)
    got_relay = to(far.at[up_slot, rows_of(2)], relay, y_up)
    down_slot = jnp.where((y + 3) % 4 < 2, B, C)
    got_d = [to(far.at[down_slot, rows_of(k)], far.at[D, rows_of(k)], y_down) for k in range(2)]
    got_d.append(to(relay, far.at[D, rows_of(2)], y_up))

    def pass_c(k):
        got_b[k].wait_recv()
        got_c[k].start()

    def pass_d(k):
        got_c[k].wait_recv()
        got_d[k].start()

    pass_c(0)
    got_a[2].wait_recv()
    got_relay.start()
    half = TIMES // 2
    t_mine, t_other = z_lo * half, (1 - z_lo) * half

    def half_tile(n, carry):
        @pl.when(n == 1)
        def _():
            got_relay.wait_recv()
            got_d[2].start()
            pass_d(0)
        tile(n, half)
        return carry

    def step(n, carry):
        slot, column = n // 3, n % 3

        @pl.when(n == 1)
        def _():
            got_own.wait_recv()

        @pl.when(n == 3)
        def _():
            pass_c(1)
            got_a[1].wait_recv()
            got_a[0].wait_recv()
            scale(A, t_mine, half)
            lax.fori_loop(0, 3, half_tile, 0)
            apply(A, t_mine, half)
            applied[pl.ds(t_other, half), A * SLAB:(A + 1) * SLAB, :] = jnp.zeros((half, SLAB, N_POT), F32)
            pass_c(2)

        @pl.when(n == 4)
        def _():
            pass_d(1)

        @pl.when(n == 6)
        def _():
            got_c[2].wait_recv()

        @pl.when(n == 9)
        def _():
            for k in (2, 0, 1):
                got_d[k].wait_recv()

        @pl.when(column == 0)
        def _():
            scale(slot, 0, TIMES)

        tile(column, TIMES)

        @pl.when(column == 2)
        def _():
            apply(slot, 0, TIMES)
        return carry

    lax.fori_loop(0, 12, step, 0)

    pot_far[0:SLAB] = far[OWN, :, N_ORB:] * jnp.asarray(0.5, BF16)
    for slot in (B, C, D, A):
        pot_far[slot * SLAB:(slot + 1) * SLAB] = far[slot, :, N_ORB:]
    used = 5 * SLAB
    pot_far[used:] = jnp.zeros((N_POT - used, N_POT), BF16)
    pot_t = pot_far[...].T
    applied[:, used:, :] = jnp.zeros((TIMES, N_POT - used, N_POT), F32)

    def project(t, carry):
        whole = applied[t]
        high = whole.astype(BF16)
        low = (whole - high.astype(F32)).astype(BF16)
        both = jnp.dot(pot_t, high, preferred_element_type=F32) + jnp.dot(
            pot_t, low, preferred_element_type=F32)
        proj[t, 0:128] = both[:128, :128]
        proj[t, 128:256] = both[:128, 128:] + both[128:, :128].T
        proj[t, 256:384] = both[128:, 128:]
        return carry

    lax.fori_loop(0, TIMES, project, 0)

    def combine(a, w, carry):
        w_zh, w_x = w // 4, w % 4
        weight = [tw_all[tw_at(t), pl.ds(w, 1), :] for t in range(TIMES)]
        for h in range(2):
            for zl in range(2):
                for yy in range(4):
                    rows = pl.ds(((h * 3 + a) * 8 + zl * 4 + yy) * 8, 8)
                    total = weight[0] * proj[0, rows]
                    for t in range(1, TIMES):
                        total = total + weight[t] * proj[t, rows]
                    zz = w_zh * 2 + zl
                    place = ((w_x, yy, zz), (yy, zz, w_x), (zz, w_x, yy))[a]
                    sums[h, a, place[0], place[1], place[2]] = total
        return carry

    swaps = []
    for a in range(3):
        lax.fori_loop(0, TIMES, functools.partial(combine, a), 0)
        swap = pltpu.make_async_remote_copy(
            src_ref=sums.at[1 - core, a], dst_ref=from_core.at[a],
            send_sem=core_sem.at[a], recv_sem=core_sem.at[3 + a],
            device_id=sibling, device_id_type=MESH)
        swap.start()
        swaps.append(swap)
    z = z_hi * 2 + z_lo
    place = (x, y, z)

    def along(axis, index):
        if axis == 0:
            return (pts, z_hi * 4 + index)
        if axis == 1:
            return at(y_=index)
        return at(z_lo_=index % 2, z_hi_=index // 2)

    copies = []
    held = from_core
    wave = [[swap] for swap in swaps]
    for stage, (arrive, left) in enumerate(((arrive1, left1), (arrive2, left2), (arrive3, final), (None, None))):
        fresh = []
        for a in range(3):
            for copy in wave[a]:
                copy.wait_recv()
            if stage == 0:
                from_core[a] = from_core[a] + sums[core, a]
            else:
                source, landed, total = last
                total[a] = source[a, place[(a + stage - 1) % 3]] + landed[a, 0] + landed[a, 1] + landed[a, 2]
            if arrive is None:
                continue
            axis = (a + stage) % 3
            sends = []
            for d in (2, 1, 3):
                index = (place[axis] + d) % 4
                i = (stage * 3 + a) * 3 + d - 1
                copy = pltpu.make_async_remote_copy(
                    src_ref=held.at[a, index], dst_ref=arrive.at[a, d - 1],
                    send_sem=ring_send.at[i], recv_sem=ring_recv.at[i],
                    device_id=along(axis, index), device_id_type=MESH)
                copy.start()
                sends.append(copy)
            fresh.append(sends)
            copies += sends
        wave, last, held = fresh, (held, arrive, left), left

    def spread(i, src, dst, peer):
        copy = pltpu.make_async_remote_copy(
            src_ref=src, dst_ref=dst, send_sem=all_send.at[i], recv_sem=all_recv.at[i],
            device_id=peer, device_id_type=MESH)
        copy.start()
        return copy

    corner = z_lo * 2 + core
    near = [spread(i, final, quad.at[corner], peer) for i, peer in enumerate((z_in_sibling, z_in, sibling))]
    quad[corner] = final[...]
    for copy in near:
        copy.wait_recv()
    wide = [spread(3 + i, quad, whole_out.at[y], peer) for i, peer in enumerate((y_across, y_up, y_down))]
    whole_out[y] = quad[...]
    for copy in wide:
        copy.wait_recv()
    rows = []
    for h in range(2):
        for a in range(3):
            for zl in range(2):
                for yy in range(4):
                    rows.append(whole_out[yy, zl * 2 + h, a])
    low, mid, high = [jnp.concatenate(rows[16 * b:16 * b + 16], axis=0) for b in range(3)]
    out_ref[0, :128, :128] = low + low.T
    out_ref[0, :128, 128:] = mid
    out_ref[0, 128:, :128] = mid.T
    out_ref[0, 128:, 128:] = high + high.T
    for copy in sent + tw_copies + swaps + copies + near + wide:
        copy.wait_send()


def body(occ, virt, pot, occ_energy, virt_energy, times, weights):
    anywhere, vmem = pl.BlockSpec(memory_space=pl.ANY), pl.BlockSpec(memory_space=pltpu.VMEM)
    smem = pl.BlockSpec(memory_space=pltpu.SMEM)
    return pl.pallas_call(
        kernel,
        out_shape=jax.ShapeDtypeStruct((1, N_POT, N_POT), F32),
        in_specs=[anywhere] * 3 + [vmem] * 2 + [smem] * 2,
        out_specs=vmem,
        scratch_shapes=[
            pltpu.VMEM((2 * ROWS, WIDTH), BF16),
            pltpu.VMEM((5, SLAB, WIDTH), BF16),
            pltpu.VMEM((CHUNK, WIDTH), BF16),
            pltpu.VMEM((TIMES * SLAB, N_ORB), BF16),
            pltpu.VMEM((TIMES * SLAB, 2 * ROWS), BF16),
            pltpu.VMEM((TIMES, N_POT, N_POT), F32),
            pltpu.VMEM((TIMES, 1, N_ORB), F32),
            pltpu.VMEM((TIMES, 16, 128), F32),
            pltpu.VMEM((N_POT, N_POT), BF16),
            pltpu.VMEM((TIMES, 384, 128), F32),
            pltpu.VMEM((2, 3, 4, 4, 4, 8, 128), F32),
            pltpu.VMEM((3, 4, 4, 4, 8, 128), F32),
            pltpu.VMEM((3, 3, 4, 4, 8, 128), F32),
            pltpu.VMEM((3, 3, 4, 8, 128), F32),
            pltpu.VMEM((3, 3, 8, 128), F32),
            pltpu.VMEM((3, 4, 4, 8, 128), F32),
            pltpu.VMEM((3, 4, 8, 128), F32),
            pltpu.VMEM((3, 8, 128), F32),
            pltpu.VMEM((4, 3, 8, 128), F32),
            pltpu.VMEM((4, 4, 3, 8, 128), F32),
            pltpu.SemaphoreType.DMA((6,)),
            pltpu.SemaphoreType.DMA((24,)),
            pltpu.SemaphoreType.DMA((24,)),
            pltpu.SemaphoreType.DMA((4,)),
            pltpu.SemaphoreType.DMA((4,)),
            pltpu.SemaphoreType.DMA((6,)),
            pltpu.SemaphoreType.DMA((27,)),
            pltpu.SemaphoreType.DMA((27,)),
            pltpu.SemaphoreType.DMA((6,)),
            pltpu.SemaphoreType.DMA((6,)),
        ],
        compiler_params=pltpu.CompilerParams(
            collective_id=0, has_side_effects=True, vmem_limit_bytes=60 * 2**20),
    )(occ, virt, pot, occ_energy[None, :], virt_energy[None, :], times, weights.T)


def solution(mesh):
    return jax.shard_map(
        body,
        mesh=mesh,
        in_specs=(P("pts", None), P("pts", None), P("pts", None), P(), P(), P("tau"), P(None, "tau")),
        out_specs=P("tau", None, None),
        check_vma=False,
    )
```

```python
import functools

import jax
import jax.numpy as jnp
from jax import lax
from jax.experimental import pallas as pl
from jax.experimental.pallas import tpu as pltpu
from jax.sharding import PartitionSpec as P

MESH = pl.DeviceIdType.MESH
NT = (((1,), (1,)), ((), ()))
N_OCC, N_VIRT, N_POT, ROWS = 2048, 4096, 256, 384
N_ORB = N_OCC + N_VIRT
WIDTH = N_ORB + N_POT
TIMES = 8
SLAB = ROWS // TIMES
CHUNK = 16
CHUNKS = SLAB // CHUNK
OWN, B, C, D, A = range(5)
F32, BF16 = jnp.float32, jnp.bfloat16


def kernel(
    occ_ref, virt_ref, pot_ref, occ_e_ref, virt_e_ref, times_ref, weights_ref, out_ref,
    own, far, relay, scaled, resp, applied, factor, tw_all, pot_far, proj,
    sums, from_core, arrive1, arrive2, left1, final, whole_out,
    load_sem, send_sem, recv_sem, tw_send, tw_recv,
    core_sem, ring_send, ring_recv, plane_sem, all_send, all_recv,
):
    pts, tau = lax.axis_index("pts"), lax.axis_index("tau")
    z_lo, y, core = pts // 8, (pts // 2) % 4, pts % 2
    z_hi, x = tau // 4, tau % 4

    def at(z_lo_=None, y_=None, core_=None, z_hi_=None):
        zl = z_lo if z_lo_ is None else z_lo_
        yy = y if y_ is None else y_
        cc = core if core_ is None else core_
        zh = z_hi if z_hi_ is None else z_hi_
        return (zl * 8 + yy * 2 + cc, zh * 4 + x)

    sibling = at(core_=1 - core)
    z_out = at(z_lo_=1 - z_lo, z_hi_=1 - z_hi)
    z_in = at(z_lo_=1 - z_lo)
    y_down = at(y_=(y + 3) % 4)
    y_up = at(y_=(y + 1) % 4)
    tau_peers = [(pts, (tau + d) % TIMES) for d in range(1, TIMES)]
    place = (x, y, z_hi * 2 + z_lo)

    def device(x_, y_, z_):
        return ((z_ % 2) * 8 + y_ * 2 + core, (z_ // 2) * 4 + x_)

    def off(*steps):
        return device(*[(p + d) % 4 for p, d in zip(place, steps)])

    in_planes = [
        off(i // 16, i // 4 % 4, i % 4) for i in range(1, 64) if 0 in (i // 16, i // 4 % 4, i % 4)]

    first = pl.multiple_of(tau * SLAB, CHUNK)
    parts = ((occ_ref, 0, N_OCC), (virt_ref, N_OCC, N_VIRT), (pot_ref, N_ORB, N_POT))
    loads = []
    for i, (ref, at_col, cols) in enumerate(parts):
        loads.append(pltpu.make_async_copy(
            ref.at[pl.ds(first, SLAB)], far.at[OWN, :, pl.ds(at_col, cols)], load_sem.at[i]))
    for i, (ref, at_col, cols) in enumerate(parts):
        loads.append(pltpu.make_async_copy(
            ref, own.at[pl.ds(0, ROWS), pl.ds(at_col, cols)], load_sem.at[3 + i]))
    for load in loads:
        load.start()

    barrier = pltpu.get_barrier_semaphore()
    greeted = [sibling] + in_planes
    for peer in greeted:
        pl.semaphore_signal(barrier, 1, device_id=peer, device_id_type=MESH)
    for w in range(TIMES):
        tw_all[tau, w:w + 1] = jnp.full((1, 128), weights_ref[0, w], F32)
    tw_all[tau, 8:16] = jnp.full((8, 128), times_ref[0], F32)
    pl.semaphore_wait(barrier, len(greeted))

    count = iter(range(64))
    sent = []

    def to(src, dst, peer):
        i = next(count)
        copy = pltpu.make_async_remote_copy(
            src_ref=src, dst_ref=dst, send_sem=send_sem.at[i], recv_sem=recv_sem.at[i],
            device_id=peer, device_id_type=MESH)
        sent.append(copy)
        return copy

    def send(src, dst, peer):
        copy = to(src, dst, peer)
        copy.start()
        return copy

    tw_copies = []
    for i, peer in enumerate(tau_peers):
        copy = pltpu.make_async_remote_copy(
            src_ref=tw_all.at[tau], dst_ref=tw_all.at[tau], send_sem=tw_send.at[i], recv_sem=tw_recv.at[i],
            device_id=peer, device_id_type=MESH)
        copy.start()
        tw_copies.append(copy)

    def rows_of(k):
        return pl.ds(k * CHUNK, CHUNK)

    for load in loads[:3]:
        load.wait()
    got_b = [send(far.at[OWN, rows_of(k)], far.at[B, rows_of(k)], y_down) for k in range(CHUNKS)]
    for load in loads[3:]:
        load.wait()
    out_first = ((1 - z_hi) * 4 + x) * SLAB

    def own_rows(start, k):
        return own.at[pl.ds(pl.multiple_of(start + k * CHUNK, CHUNK), CHUNK)]

    got_a = {
        2: send(own_rows(first, 2), far.at[A, rows_of(2)], z_in),
        1: send(own_rows(out_first, 1), far.at[A, rows_of(1)], z_out),
        0: send(own_rows(out_first, 0), far.at[A, rows_of(0)], z_out),
    }
    got_own = send(own.at[pl.ds(0, ROWS)], own.at[pl.ds(ROWS, ROWS)], sibling)

    for copy in tw_copies:
        copy.wait_recv()
    for t in range(TIMES):
        moment = tw_all[t, 8:9, 0:1]
        factor[t, :, :N_OCC] = jnp.exp(moment * occ_e_ref[...])
        factor[t, :, N_OCC:] = jnp.exp(-moment * virt_e_ref[...])

    def scale(slot, t_first, t_count):
        def one(i, carry):
            rows = pl.ds(pl.multiple_of((i % CHUNKS) * CHUNK, CHUNK), CHUNK)
            wide = far[slot, rows, pl.ds(0, N_ORB)].astype(F32) * factor[t_first + i // CHUNKS]
            scaled[pl.ds(pl.multiple_of(i * CHUNK, CHUNK), CHUNK)] = wide.astype(BF16)
            return carry
        lax.fori_loop(0, t_count * CHUNKS, one, 0)

    def tile(n, t_count):
        lines = t_count * SLAB
        n0 = pl.multiple_of(n * 256, 256)
        g_occ = lax.dot_general(
            scaled[:lines, :N_OCC], own[pl.ds(n0, 256), :N_OCC], NT, preferred_element_type=F32)
        g_virt = lax.dot_general(
            scaled[:lines, N_OCC:], own[pl.ds(n0, 256), N_OCC:N_ORB], NT, preferred_element_type=F32)
        resp[:lines, pl.ds(n0, 256)] = (-(g_occ * g_virt)).astype(BF16)

    def apply(slot, t_first, t_count):
        lines = t_count * SLAB
        part = jnp.dot(resp[:lines], own[:, N_ORB:], preferred_element_type=F32)
        rows = pl.ds(pl.multiple_of(slot * SLAB, CHUNK), SLAB)
        applied[pl.ds(t_first, t_count), rows, :] = part.reshape(t_count, SLAB, N_POT)

    got_c = [to(far.at[B, rows_of(k)], far.at[C, rows_of(k)], z_in) for k in range(CHUNKS)]
    up_slot = jnp.where((y + 2) % 4 < 2, OWN, A)
    got_relay = to(far.at[up_slot, rows_of(2)], relay, y_up)
    down_slot = jnp.where((y + 3) % 4 < 2, B, C)
    got_d = [to(far.at[down_slot, rows_of(k)], far.at[D, rows_of(k)], y_down) for k in range(2)]
    got_d.append(to(relay, far.at[D, rows_of(2)], y_up))

    def pass_c(k):
        got_b[k].wait_recv()
        got_c[k].start()

    def pass_d(k):
        got_c[k].wait_recv()
        got_d[k].start()

    pass_c(0)
    got_a[2].wait_recv()
    got_relay.start()
    half = TIMES // 2
    t_mine, t_other = z_lo * half, (1 - z_lo) * half

    def half_tile(n, carry):
        @pl.when(n == 1)
        def _():
            got_relay.wait_recv()
            got_d[2].start()
            pass_d(0)
        tile(n, half)
        return carry

    def full_tile(slot, column, carry):
        @pl.when((slot == OWN) & (column == 1))
        def _():
            got_own.wait_recv()

        @pl.when((slot == B) & (column == 1))
        def _():
            pass_d(1)

        tile(column, TIMES)
        return carry

    def step(slot, carry):
        @pl.when(slot == B)
        def _():
            pass_c(1)
            got_a[1].wait_recv()
            got_a[0].wait_recv()
            scale(A, t_mine, half)
            lax.fori_loop(0, 3, half_tile, 0)
            apply(A, t_mine, half)
            applied[pl.ds(t_other, half), A * SLAB:(A + 1) * SLAB, :] = jnp.zeros((half, SLAB, N_POT), F32)
            pass_c(2)

        @pl.when(slot == C)
        def _():
            got_c[2].wait_recv()

        @pl.when(slot == D)
        def _():
            for k in (2, 0, 1):
                got_d[k].wait_recv()

        scale(slot, 0, TIMES)
        lax.fori_loop(0, 3, functools.partial(full_tile, slot), 0)
        apply(slot, 0, TIMES)
        return carry

    lax.fori_loop(0, 4, step, 0)

    pot_far[0:SLAB] = far[OWN, :, N_ORB:] * jnp.asarray(0.5, BF16)
    for slot in (B, C, D, A):
        pot_far[slot * SLAB:(slot + 1) * SLAB] = far[slot, :, N_ORB:]
    used = 5 * SLAB
    pot_far[used:] = jnp.zeros((N_POT - used, N_POT), BF16)
    pot_t = pot_far[...].T
    applied[:, used:, :] = jnp.zeros((TIMES, N_POT - used, N_POT), F32)

    def project(t, carry):
        whole = applied[t]
        high = whole.astype(BF16)
        low = (whole - high.astype(F32)).astype(BF16)
        both = jnp.dot(pot_t, high, preferred_element_type=F32) + jnp.dot(
            pot_t, low, preferred_element_type=F32)
        proj[t, 0:128] = both[:128, :128]
        proj[t, 128:256] = both[:128, 128:] + both[128:, :128].T
        proj[t, 256:384] = both[128:, 128:]
        return carry

    lax.fori_loop(0, TIMES, project, 0)

    def combine(h, a, w, carry):
        w_zh, w_x = w // 4, w % 4
        weight = [tw_all[t, pl.ds(w, 1), :] for t in range(TIMES)]
        for zl in range(2):
            for yy in range(4):
                rows = pl.ds(pl.multiple_of(((h * 3 + a) * 8 + zl * 4 + yy) * 8, 8), 8)
                total = weight[0] * proj[0, rows]
                for t in range(1, TIMES):
                    total = total + weight[t] * proj[t, rows]
                zz = w_zh * 2 + zl
                spot = ((w_x, yy, zz), (yy, zz, w_x), (zz, w_x, yy))[a]
                sums[h, a, spot[0], spot[1], spot[2]] = total
        return carry

    swaps = []
    for a in range(3):
        lax.fori_loop(0, TIMES, functools.partial(combine, 1 - core, a), 0)
        swap = pltpu.make_async_remote_copy(
            src_ref=sums.at[1 - core, a], dst_ref=from_core.at[a],
            send_sem=core_sem.at[a], recv_sem=core_sem.at[3 + a],
            device_id=sibling, device_id_type=MESH)
        swap.start()
        swaps.append(swap)
    copies = []
    wave = []
    for a in range(3):
        lax.fori_loop(0, TIMES, functools.partial(combine, core, a), 0)
        swaps[a].wait_recv()
        from_core[a] = from_core[a] + sums[core, a]
        sends = []
        for d in (2, 1, 3):
            index = (place[a] + d) % 4
            i = a * 3 + d - 1
            copy = pltpu.make_async_remote_copy(
                src_ref=from_core.at[a, index], dst_ref=arrive1.at[a, d - 1],
                send_sem=ring_send.at[i], recv_sem=ring_recv.at[i],
                device_id=device(*[index if k == a else place[k] for k in range(3)]), device_id_type=MESH)
            copy.start()
            sends.append(copy)
        wave.append(sends)
        copies += sends
    planes = []
    for a in range(3):
        for copy in wave[a]:
            copy.wait_recv()
        left1[a] = from_core[a, place[a]] + arrive1[a, 0] + arrive1[a, 1] + arrive1[a, 2]

        def fan(d, carry):
            spot = list(place)
            second, third = (a + 1) % 3, (a + 2) % 3
            spot[second] = (place[second] + d // 4) % 4
            spot[third] = (place[third] + d % 4) % 4
            pltpu.make_async_remote_copy(
                src_ref=left1.at[a, spot[second], spot[third]], dst_ref=arrive2.at[a, d - 1],
                send_sem=plane_sem.at[a], recv_sem=plane_sem.at[3 + a],
                device_id=device(*spot), device_id_type=MESH).start()
            return carry

        lax.fori_loop(1, 16, fan, 0)
        planes.append(pltpu.make_async_remote_copy(
            src_ref=arrive2.at[a], dst_ref=arrive2.at[a], send_sem=plane_sem.at[a],
            recv_sem=plane_sem.at[3 + a], device_id=sibling, device_id_type=MESH))
    for a in range(3):
        planes[a].wait_recv()
        total = left1[a, place[(a + 1) % 3], place[(a + 2) % 3]]
        for d in range(15):
            total = total + arrive2[a, d]
        final[a] = total

    def spread(i, src, dst, peer):
        copy = pltpu.make_async_remote_copy(
            src_ref=src, dst_ref=dst, send_sem=all_send.at[i], recv_sem=all_recv.at[i],
            device_id=peer, device_id_type=MESH)
        copy.start()
        return copy

    corner = z_lo * 4 + y
    wide = [
        spread(i, final, whole_out.at[core, corner], at(z_lo_=(z_lo + (i + 1) // 4) % 2, y_=(y + (i + 1) % 4) % 4))
        for i in range(7)]
    whole_out[core, corner] = final[...]
    for copy in wide:
        copy.wait_recv()
    near = [spread(7, whole_out.at[core], whole_out.at[core], sibling)]
    near[0].wait_recv()
    rows = []
    for h in range(2):
        for a in range(3):
            for zl in range(2):
                for yy in range(4):
                    rows.append(whole_out[h, zl * 4 + yy, a])
    low, mid, high = [jnp.concatenate(rows[16 * b:16 * b + 16], axis=0) for b in range(3)]
    out_ref[0, :128, :128] = low + low.T
    out_ref[0, :128, 128:] = mid
    out_ref[0, 128:, :128] = mid.T
    out_ref[0, 128:, 128:] = high + high.T
    for copy in sent + tw_copies + swaps + copies + planes + near + wide:
        copy.wait_send()


def body(occ, virt, pot, occ_energy, virt_energy, times, weights):
    anywhere, vmem = pl.BlockSpec(memory_space=pl.ANY), pl.BlockSpec(memory_space=pltpu.VMEM)
    smem = pl.BlockSpec(memory_space=pltpu.SMEM)
    return pl.pallas_call(
        kernel,
        out_shape=jax.ShapeDtypeStruct((1, N_POT, N_POT), F32),
        in_specs=[anywhere] * 3 + [vmem] * 2 + [smem] * 2,
        out_specs=vmem,
        scratch_shapes=[
            pltpu.VMEM((2 * ROWS, WIDTH), BF16),
            pltpu.VMEM((5, SLAB, WIDTH), BF16),
            pltpu.VMEM((CHUNK, WIDTH), BF16),
            pltpu.VMEM((TIMES * SLAB, N_ORB), BF16),
            pltpu.VMEM((TIMES * SLAB, 2 * ROWS), BF16),
            pltpu.VMEM((TIMES, N_POT, N_POT), F32),
            pltpu.VMEM((TIMES, 1, N_ORB), F32),
            pltpu.VMEM((TIMES, 16, 128), F32),
            pltpu.VMEM((N_POT, N_POT), BF16),
            pltpu.VMEM((TIMES, 384, 128), F32),
            pltpu.VMEM((2, 3, 4, 4, 4, 8, 128), F32),
            pltpu.VMEM((3, 4, 4, 4, 8, 128), F32),
            pltpu.VMEM((3, 3, 4, 4, 8, 128), F32),
            pltpu.VMEM((3, 15, 8, 128), F32),
            pltpu.VMEM((3, 4, 4, 8, 128), F32),
            pltpu.VMEM((3, 8, 128), F32),
            pltpu.VMEM((2, 8, 3, 8, 128), F32),
            pltpu.SemaphoreType.DMA((6,)),
            pltpu.SemaphoreType.DMA((24,)),
            pltpu.SemaphoreType.DMA((24,)),
            pltpu.SemaphoreType.DMA((7,)),
            pltpu.SemaphoreType.DMA((7,)),
            pltpu.SemaphoreType.DMA((6,)),
            pltpu.SemaphoreType.DMA((9,)),
            pltpu.SemaphoreType.DMA((9,)),
            pltpu.SemaphoreType.DMA((6,)),
            pltpu.SemaphoreType.DMA((8,)),
            pltpu.SemaphoreType.DMA((8,)),
        ],
        compiler_params=pltpu.CompilerParams(
            collective_id=0, has_side_effects=True, vmem_limit_bytes=60 * 2**20),
    )(occ, virt, pot, occ_energy[None, :], virt_energy[None, :], times, weights.T)


def solution(mesh):
    return jax.shard_map(
        body,
        mesh=mesh,
        in_specs=(P("pts", None), P("pts", None), P("pts", None), P(), P(), P("tau"), P(None, "tau")),
        out_specs=P("tau", None, None),
        check_vma=False,
    )
```

```python
import functools

import jax
import jax.numpy as jnp
from jax import lax
from jax.experimental import pallas as pl
from jax.experimental.pallas import tpu as pltpu
from jax.sharding import PartitionSpec as P

MESH = pl.DeviceIdType.MESH
NT = (((1,), (1,)), ((), ()))
N_OCC, N_VIRT, N_POT, ROWS = 2048, 4096, 256, 384
N_ORB = N_OCC + N_VIRT
WIDTH = N_ORB + N_POT
TIMES = 8
SLAB = ROWS // TIMES
CHUNK = 16
CHUNKS = SLAB // CHUNK
OWN, B, C, D, A = range(5)
F32, BF16 = jnp.float32, jnp.bfloat16


def kernel(
    occ_ref, virt_ref, pot_ref, occ_e_ref, virt_e_ref, times_ref, weights_ref, out_ref,
    own, far, relay, scaled, resp, applied, factor, tw_all, pot_far, proj,
    sums, from_core, arrive1, arrive2, left1, final, whole_out,
    load_sem, send_sem, recv_sem, tw_send, tw_recv,
    core_sem, ring_send, ring_recv, plane_sem, all_send, all_recv,
):
    pts, tau = lax.axis_index("pts"), lax.axis_index("tau")
    z_lo, y, core = pts // 8, (pts // 2) % 4, pts % 2
    z_hi, x = tau // 4, tau % 4

    def at(z_lo_=None, y_=None, core_=None, z_hi_=None):
        zl = z_lo if z_lo_ is None else z_lo_
        yy = y if y_ is None else y_
        cc = core if core_ is None else core_
        zh = z_hi if z_hi_ is None else z_hi_
        return (zl * 8 + yy * 2 + cc, zh * 4 + x)

    sibling = at(core_=1 - core)
    z_out = at(z_lo_=1 - z_lo, z_hi_=1 - z_hi)
    z_in = at(z_lo_=1 - z_lo)
    y_down = at(y_=(y + 3) % 4)
    y_up = at(y_=(y + 1) % 4)
    tau_peers = [
        (pts, ((z_hi + dz) % 2) * 4 + (x + dx) % 4)
        for dz, dx in ((1, 2), (1, 1), (1, 3), (1, 0), (0, 2), (0, 1), (0, 3))]
    place = (x, y, z_hi * 2 + z_lo)

    ahead = [[lax.rem(p + d, 4) for d in range(4)] for p in place]
    in_pts = [[0] * 4, [2 * c + core for c in ahead[1]], [8 * lax.rem(c, 2) for c in ahead[2]]]
    in_tau = [ahead[0], [0] * 4, [4 * lax.div(c, 2) for c in ahead[2]]]

    def off(*steps):
        return (in_pts[1][steps[1]] + in_pts[2][steps[2]], in_tau[0][steps[0]] + in_tau[2][steps[2]])

    in_planes = [
        off(i // 16, i // 4 % 4, i % 4) for i in range(1, 64) if 0 in (i // 16, i // 4 % 4, i % 4)]

    first = pl.multiple_of(tau * SLAB, CHUNK)
    parts = ((occ_ref, 0, N_OCC), (virt_ref, N_OCC, N_VIRT), (pot_ref, N_ORB, N_POT))
    loads = []
    for i, (ref, at_col, cols) in enumerate(parts):
        loads.append(pltpu.make_async_copy(
            ref.at[pl.ds(first, SLAB)], far.at[OWN, :, pl.ds(at_col, cols)], load_sem.at[i]))
    for i, (ref, at_col, cols) in enumerate(parts):
        loads.append(pltpu.make_async_copy(
            ref, own.at[pl.ds(0, ROWS), pl.ds(at_col, cols)], load_sem.at[3 + i]))
    for load in loads:
        load.start()

    barrier = pltpu.get_barrier_semaphore()
    greeted = [sibling] + in_planes
    for peer in greeted:
        pl.semaphore_signal(barrier, 1, device_id=peer, device_id_type=MESH)
    for w in range(TIMES):
        tw_all[tau, w:w + 1] = jnp.full((1, 128), weights_ref[0, w], F32)
    tw_all[tau, 8:16] = jnp.full((8, 128), times_ref[0], F32)
    pl.semaphore_wait(barrier, len(greeted))

    count = iter(range(64))
    sent = []

    def to(src, dst, peer):
        i = next(count)
        copy = pltpu.make_async_remote_copy(
            src_ref=src, dst_ref=dst, send_sem=send_sem.at[i], recv_sem=recv_sem.at[i],
            device_id=peer, device_id_type=MESH)
        sent.append(copy)
        return copy

    def send(src, dst, peer):
        copy = to(src, dst, peer)
        copy.start()
        return copy

    tw_copies = []
    for i, peer in enumerate(tau_peers):
        copy = pltpu.make_async_remote_copy(
            src_ref=tw_all.at[tau], dst_ref=tw_all.at[tau], send_sem=tw_send.at[i], recv_sem=tw_recv.at[i],
            device_id=peer, device_id_type=MESH)
        copy.start()
        tw_copies.append(copy)

    def rows_of(k):
        return pl.ds(k * CHUNK, CHUNK)

    for load in loads[:3]:
        load.wait()
    got_b = [send(far.at[OWN, rows_of(k)], far.at[B, rows_of(k)], y_down) for k in range(CHUNKS)]
    for load in loads[3:]:
        load.wait()
    out_first = ((1 - z_hi) * 4 + x) * SLAB

    def own_rows(start, k):
        return own.at[pl.ds(pl.multiple_of(start + k * CHUNK, CHUNK), CHUNK)]

    got_a = {
        2: send(own_rows(first, 2), far.at[A, rows_of(2)], z_in),
        1: send(own_rows(out_first, 1), far.at[A, rows_of(1)], z_out),
        0: send(own_rows(out_first, 0), far.at[A, rows_of(0)], z_out),
    }
    got_own = send(own.at[pl.ds(0, ROWS)], own.at[pl.ds(ROWS, ROWS)], sibling)

    for copy in tw_copies:
        copy.wait_recv()
    for t in range(TIMES):
        moment = tw_all[t, 8:9, 0:1]
        factor[t, :, :N_OCC] = jnp.exp(moment * occ_e_ref[...])
        factor[t, :, N_OCC:] = jnp.exp(-moment * virt_e_ref[...])

    def scale(slot, t_first, t_count):
        def one(i, carry):
            rows = pl.ds(pl.multiple_of((i % CHUNKS) * CHUNK, CHUNK), CHUNK)
            wide = far[slot, rows, pl.ds(0, N_ORB)].astype(F32) * factor[t_first + i // CHUNKS]
            scaled[pl.ds(pl.multiple_of(i * CHUNK, CHUNK), CHUNK)] = wide.astype(BF16)
            return carry
        lax.fori_loop(0, t_count * CHUNKS, one, 0)

    def tile(n, t_count):
        lines = t_count * SLAB
        n0 = pl.multiple_of(n * 256, 256)
        g_occ = lax.dot_general(
            scaled[:lines, :N_OCC], own[pl.ds(n0, 256), :N_OCC], NT, preferred_element_type=F32)
        g_virt = lax.dot_general(
            scaled[:lines, N_OCC:], own[pl.ds(n0, 256), N_OCC:N_ORB], NT, preferred_element_type=F32)
        resp[:lines, pl.ds(n0, 256)] = (-(g_occ * g_virt)).astype(BF16)

    def apply(slot, t_first, t_count):
        lines = t_count * SLAB
        part = jnp.dot(resp[:lines], own[:, N_ORB:], preferred_element_type=F32)
        rows = pl.ds(pl.multiple_of(slot * SLAB, CHUNK), SLAB)
        applied[pl.ds(t_first, t_count), rows, :] = part.reshape(t_count, SLAB, N_POT)

    got_c = [to(far.at[B, rows_of(k)], far.at[C, rows_of(k)], z_in) for k in range(CHUNKS)]
    up_slot = jnp.where((y + 2) % 4 < 2, OWN, A)
    got_relay = to(far.at[up_slot, rows_of(2)], relay, y_up)
    down_slot = jnp.where((y + 3) % 4 < 2, B, C)
    got_d = [to(far.at[down_slot, rows_of(k)], far.at[D, rows_of(k)], y_down) for k in range(2)]
    got_d.append(to(relay, far.at[D, rows_of(2)], y_up))

    def pass_c(k):
        got_b[k].wait_recv()
        got_c[k].start()

    def pass_d(k):
        got_c[k].wait_recv()
        got_d[k].start()

    pass_c(0)
    got_a[2].wait_recv()
    got_relay.start()
    half = TIMES // 2
    t_mine, t_other = z_lo * half, (1 - z_lo) * half

    def half_tile(n, carry):
        @pl.when(n == 1)
        def _():
            got_relay.wait_recv()
            got_d[2].start()
            pass_d(0)
        tile(n, half)
        return carry

    def full_tile(slot, column, carry):
        @pl.when((slot == OWN) & (column == 1))
        def _():
            got_own.wait_recv()

        @pl.when((slot == B) & (column == 1))
        def _():
            pass_d(1)

        tile(column, TIMES)
        return carry

    def step(slot, carry):
        @pl.when(slot == B)
        def _():
            pass_c(1)
            got_a[1].wait_recv()
            got_a[0].wait_recv()
            scale(A, t_mine, half)
            lax.fori_loop(0, 3, half_tile, 0)
            apply(A, t_mine, half)
            applied[pl.ds(t_other, half), A * SLAB:(A + 1) * SLAB, :] = jnp.zeros((half, SLAB, N_POT), F32)
            pass_c(2)

        @pl.when(slot == C)
        def _():
            got_c[2].wait_recv()

        @pl.when(slot == D)
        def _():
            for k in (2, 0, 1):
                got_d[k].wait_recv()

        scale(slot, 0, TIMES)
        lax.fori_loop(0, 3, functools.partial(full_tile, slot), 0)
        apply(slot, 0, TIMES)
        return carry

    lax.fori_loop(0, 4, step, 0)

    pot_far[0:SLAB] = far[OWN, :, N_ORB:] * jnp.asarray(0.5, BF16)
    for slot in (B, C, D, A):
        pot_far[slot * SLAB:(slot + 1) * SLAB] = far[slot, :, N_ORB:]
    used = 5 * SLAB
    pot_far[used:] = jnp.zeros((N_POT - used, N_POT), BF16)
    pot_t = pot_far[...].T
    applied[:, used:, :] = jnp.zeros((TIMES, N_POT - used, N_POT), F32)

    def project(t, carry):
        whole = applied[t]
        high = whole.astype(BF16)
        low = (whole - high.astype(F32)).astype(BF16)
        both = jnp.dot(pot_t, high, preferred_element_type=F32) + jnp.dot(
            pot_t, low, preferred_element_type=F32)
        proj[t, 0:128] = both[:128, :128]
        proj[t, 128:256] = both[:128, 128:] + both[128:, :128].T
        proj[t, 256:384] = both[128:, 128:]
        return carry

    lax.fori_loop(0, TIMES, project, 0, unroll=4)

    def combine(h, a, w, carry):
        w_zh, w_x = w // 4, w % 4
        weight = [tw_all[t, pl.ds(w, 1), :] for t in range(TIMES)]
        for zl in range(2):
            for yy in range(4):
                rows = pl.ds(pl.multiple_of(((h * 3 + a) * 8 + zl * 4 + yy) * 8, 8), 8)
                total = weight[0] * proj[0, rows]
                for t in range(1, TIMES):
                    total = total + weight[t] * proj[t, rows]
                zz = w_zh * 2 + zl
                spot = ((w_x, yy, zz), (yy, zz, w_x), (zz, w_x, yy))[a]
                sums[h, a, spot[0], spot[1], spot[2]] = total
        return carry

    swaps = []
    for a in range(3):
        lax.fori_loop(0, TIMES, functools.partial(combine, 1 - core, a), 0)
        swap = pltpu.make_async_remote_copy(
            src_ref=sums.at[1 - core, a], dst_ref=from_core.at[a],
            send_sem=core_sem.at[a], recv_sem=core_sem.at[3 + a],
            device_id=sibling, device_id_type=MESH)
        swap.start()
        swaps.append(swap)
    copies = []
    wave = []
    for a in range(3):
        lax.fori_loop(0, TIMES, functools.partial(combine, core, a), 0)
        swaps[a].wait_recv()
        from_core[a] = from_core[a] + sums[core, a]
        sends = []
        for d in (2, 1, 3):
            i = a * 3 + d - 1
            copy = pltpu.make_async_remote_copy(
                src_ref=from_core.at[a, ahead[a][d]], dst_ref=arrive1.at[a, d - 1],
                send_sem=ring_send.at[i], recv_sem=ring_recv.at[i],
                device_id=off(*[d if k == a else 0 for k in range(3)]), device_id_type=MESH)
            copy.start()
            sends.append(copy)
        wave.append(sends)
        copies += sends
    for copy in sent + tw_copies:
        copy.wait_send()
    planes = []
    for a in range(3):
        for copy in wave[a]:
            copy.wait_recv()
        left1[a] = from_core[a, place[a]] + arrive1[a, 0] + arrive1[a, 1] + arrive1[a, 2]

        second, third = (a + 1) % 3, (a + 2) % 3
        for d in range(1, 16):
            steps = [0] * 3
            steps[second], steps[third] = d // 4, d % 4
            pltpu.make_async_remote_copy(
                src_ref=left1.at[a, ahead[second][d // 4], ahead[third][d % 4]], dst_ref=arrive2.at[a, d - 1],
                send_sem=plane_sem.at[a], recv_sem=plane_sem.at[3 + a],
                device_id=off(*steps), device_id_type=MESH).start()
        planes.append(pltpu.make_async_remote_copy(
            src_ref=arrive2.at[a], dst_ref=arrive2.at[a], send_sem=plane_sem.at[a],
            recv_sem=plane_sem.at[3 + a], device_id=sibling, device_id_type=MESH))
    for a in range(3):
        planes[a].wait_recv()
        total = left1[a, place[(a + 1) % 3], place[(a + 2) % 3]]
        for d in range(15):
            total = total + arrive2[a, d]
        final[a] = total

    def spread(i, src, dst, peer):
        copy = pltpu.make_async_remote_copy(
            src_ref=src, dst_ref=dst, send_sem=all_send.at[i], recv_sem=all_recv.at[i],
            device_id=peer, device_id_type=MESH)
        copy.start()
        return copy

    corner = z_lo * 4 + y
    wide = [
        spread(i, final, whole_out.at[core, corner], at(z_lo_=(z_lo + (i + 1) // 4) % 2, y_=(y + (i + 1) % 4) % 4))
        for i in range(7)]
    whole_out[core, corner] = final[...]
    for copy in wide:
        copy.wait_recv()
    near = [spread(7, whole_out.at[core], whole_out.at[core], sibling)]
    for copy in swaps + copies + planes + wide:
        copy.wait_send()
    near[0].wait_recv()
    rows = []
    for h in range(2):
        for a in range(3):
            for zl in range(2):
                for yy in range(4):
                    rows.append(whole_out[h, zl * 4 + yy, a])
    low, mid, high = [jnp.concatenate(rows[16 * b:16 * b + 16], axis=0) for b in range(3)]
    out_ref[0, :128, :128] = low + low.T
    out_ref[0, :128, 128:] = mid
    out_ref[0, 128:, :128] = mid.T
    out_ref[0, 128:, 128:] = high + high.T
    for copy in near:
        copy.wait_send()


def body(occ, virt, pot, occ_energy, virt_energy, times, weights):
    anywhere, vmem = pl.BlockSpec(memory_space=pl.ANY), pl.BlockSpec(memory_space=pltpu.VMEM)
    smem = pl.BlockSpec(memory_space=pltpu.SMEM)
    return pl.pallas_call(
        kernel,
        out_shape=jax.ShapeDtypeStruct((1, N_POT, N_POT), F32),
        in_specs=[anywhere] * 3 + [vmem] * 2 + [smem] * 2,
        out_specs=vmem,
        scratch_shapes=[
            pltpu.VMEM((2 * ROWS, WIDTH), BF16),
            pltpu.VMEM((5, SLAB, WIDTH), BF16),
            pltpu.VMEM((CHUNK, WIDTH), BF16),
            pltpu.VMEM((TIMES * SLAB, N_ORB), BF16),
            pltpu.VMEM((TIMES * SLAB, 2 * ROWS), BF16),
            pltpu.VMEM((TIMES, N_POT, N_POT), F32),
            pltpu.VMEM((TIMES, 1, N_ORB), F32),
            pltpu.VMEM((TIMES, 16, 128), F32),
            pltpu.VMEM((N_POT, N_POT), BF16),
            pltpu.VMEM((TIMES, 384, 128), F32),
            pltpu.VMEM((2, 3, 4, 4, 4, 8, 128), F32),
            pltpu.VMEM((3, 4, 4, 4, 8, 128), F32),
            pltpu.VMEM((3, 3, 4, 4, 8, 128), F32),
            pltpu.VMEM((3, 15, 8, 128), F32),
            pltpu.VMEM((3, 4, 4, 8, 128), F32),
            pltpu.VMEM((3, 8, 128), F32),
            pltpu.VMEM((2, 8, 3, 8, 128), F32),
            pltpu.SemaphoreType.DMA((6,)),
            pltpu.SemaphoreType.DMA((24,)),
            pltpu.SemaphoreType.DMA((24,)),
            pltpu.SemaphoreType.DMA((7,)),
            pltpu.SemaphoreType.DMA((7,)),
            pltpu.SemaphoreType.DMA((6,)),
            pltpu.SemaphoreType.DMA((9,)),
            pltpu.SemaphoreType.DMA((9,)),
            pltpu.SemaphoreType.DMA((6,)),
            pltpu.SemaphoreType.DMA((8,)),
            pltpu.SemaphoreType.DMA((8,)),
        ],
        compiler_params=pltpu.CompilerParams(
            collective_id=0, has_side_effects=True, vmem_limit_bytes=60 * 2**20),
    )(occ, virt, pot, occ_energy[None, :], virt_energy[None, :], times, weights.T)


def solution(mesh):
    return jax.shard_map(
        body,
        mesh=mesh,
        in_specs=(P("pts", None), P("pts", None), P("pts", None), P(), P(), P("tau"), P(None, "tau")),
        out_specs=P("tau", None, None),
        check_vma=False,
    )
```

```python
import functools

import jax
import jax.numpy as jnp
from jax import lax
from jax.experimental import pallas as pl
from jax.experimental.pallas import tpu as pltpu
from jax.sharding import PartitionSpec as P

MESH = pl.DeviceIdType.MESH
NT = (((1,), (1,)), ((), ()))
N_OCC, N_VIRT, N_POT, ROWS = 2048, 4096, 256, 384
N_ORB = N_OCC + N_VIRT
WIDTH = N_ORB + N_POT
TIMES = 8
SLAB = ROWS // TIMES
CHUNK = 16
CHUNKS = SLAB // CHUNK
OWN, B, C, D, A = range(5)
F32, BF16 = jnp.float32, jnp.bfloat16


def kernel(
    occ_ref, virt_ref, pot_ref, occ_e_ref, virt_e_ref, times_ref, weights_ref, out_ref,
    own, far, relay, scaled, resp, applied, factor, tw_all, pot_far, proj,
    sums, from_core, arrive1, arrive2, left1, final, whole_out,
    load_sem, send_sem, recv_sem, tw_send, tw_recv,
    core_sem, ring_send, ring_recv, plane_sem, all_send, all_recv,
):
    pts, tau = lax.axis_index("pts"), lax.axis_index("tau")
    z_lo, y, core = pts // 8, (pts // 2) % 4, pts % 2
    z_hi, x = tau // 4, tau % 4

    def at(z_lo_=None, y_=None, core_=None, z_hi_=None):
        zl = z_lo if z_lo_ is None else z_lo_
        yy = y if y_ is None else y_
        cc = core if core_ is None else core_
        zh = z_hi if z_hi_ is None else z_hi_
        return (zl * 8 + yy * 2 + cc, zh * 4 + x)

    sibling = at(core_=1 - core)
    z_out = at(z_lo_=1 - z_lo, z_hi_=1 - z_hi)
    z_in = at(z_lo_=1 - z_lo)
    y_down = at(y_=(y + 3) % 4)
    y_up = at(y_=(y + 1) % 4)
    tau_peers = [
        (pts, ((z_hi + dz) % 2) * 4 + (x + dx) % 4)
        for dz, dx in ((1, 2), (1, 1), (1, 3), (1, 0), (0, 2), (0, 1), (0, 3))]
    place = (x, y, z_hi * 2 + z_lo)

    ahead = [[lax.rem(p + d, 4) for d in range(4)] for p in place]
    in_pts = [[0] * 4, [2 * c + core for c in ahead[1]], [8 * lax.rem(c, 2) for c in ahead[2]]]
    in_tau = [ahead[0], [0] * 4, [4 * lax.div(c, 2) for c in ahead[2]]]

    def off(*steps):
        return (in_pts[1][steps[1]] + in_pts[2][steps[2]], in_tau[0][steps[0]] + in_tau[2][steps[2]])

    in_planes = [
        off(i // 16, i // 4 % 4, i % 4) for i in range(1, 64) if 0 in (i // 16, i // 4 % 4, i % 4)]

    first = pl.multiple_of(tau * SLAB, CHUNK)
    parts = ((occ_ref, 0, N_OCC), (virt_ref, N_OCC, N_VIRT), (pot_ref, N_ORB, N_POT))
    loads = []
    for i, (ref, at_col, cols) in enumerate(parts):
        loads.append(pltpu.make_async_copy(
            ref.at[pl.ds(first, SLAB)], far.at[OWN, :, pl.ds(at_col, cols)], load_sem.at[i]))
    for i, (ref, at_col, cols) in enumerate(parts):
        loads.append(pltpu.make_async_copy(
            ref, own.at[pl.ds(0, ROWS), pl.ds(at_col, cols)], load_sem.at[3 + i]))
    for load in loads:
        load.start()

    barrier = pltpu.get_barrier_semaphore()
    across = [at(z_lo_=lax.rem(z_lo + d // 4, 2), y_=ahead[1][d % 4], core_=1 - core) for d in range(1, 8)]
    greeted = [sibling] + in_planes + across
    for peer in greeted:
        pl.semaphore_signal(barrier, 1, device_id=peer, device_id_type=MESH)
    for w in range(TIMES):
        tw_all[tau, w:w + 1] = jnp.full((1, 128), weights_ref[0, w], F32)
    tw_all[tau, 8:16] = jnp.full((8, 128), times_ref[0], F32)
    pl.semaphore_wait(barrier, len(greeted))

    count = iter(range(64))
    sent = []

    def to(src, dst, peer):
        i = next(count)
        copy = pltpu.make_async_remote_copy(
            src_ref=src, dst_ref=dst, send_sem=send_sem.at[i], recv_sem=recv_sem.at[i],
            device_id=peer, device_id_type=MESH)
        sent.append(copy)
        return copy

    def send(src, dst, peer):
        copy = to(src, dst, peer)
        copy.start()
        return copy

    tw_copies = []
    for i, peer in enumerate(tau_peers):
        copy = pltpu.make_async_remote_copy(
            src_ref=tw_all.at[tau], dst_ref=tw_all.at[tau], send_sem=tw_send.at[i], recv_sem=tw_recv.at[i],
            device_id=peer, device_id_type=MESH)
        copy.start()
        tw_copies.append(copy)

    def rows_of(k):
        return pl.ds(k * CHUNK, CHUNK)

    for load in loads[:3]:
        load.wait()
    got_b = [send(far.at[OWN, rows_of(k)], far.at[B, rows_of(k)], y_down) for k in range(CHUNKS)]
    for load in loads[3:]:
        load.wait()
    out_first = ((1 - z_hi) * 4 + x) * SLAB

    def own_rows(start, k):
        return own.at[pl.ds(pl.multiple_of(start + k * CHUNK, CHUNK), CHUNK)]

    got_a = {
        2: send(own_rows(first, 2), far.at[A, rows_of(2)], z_in),
        1: send(own_rows(out_first, 1), far.at[A, rows_of(1)], z_out),
        0: send(own_rows(out_first, 0), far.at[A, rows_of(0)], z_out),
    }
    got_own = send(own.at[pl.ds(0, ROWS)], own.at[pl.ds(ROWS, ROWS)], sibling)

    for copy in tw_copies:
        copy.wait_recv()
    for t in range(TIMES):
        moment = tw_all[t, 8:9, 0:1]
        factor[t, :, :N_OCC] = jnp.exp(moment * occ_e_ref[...])
        factor[t, :, N_OCC:] = jnp.exp(-moment * virt_e_ref[...])

    def scale(slot, t_first, t_count):
        def one(i, carry):
            rows = pl.ds(pl.multiple_of((i % CHUNKS) * CHUNK, CHUNK), CHUNK)
            wide = far[slot, rows, pl.ds(0, N_ORB)].astype(F32) * factor[t_first + i // CHUNKS]
            scaled[pl.ds(pl.multiple_of(i * CHUNK, CHUNK), CHUNK)] = wide.astype(BF16)
            return carry
        lax.fori_loop(0, t_count * CHUNKS, one, 0)

    def tile(n, t_count):
        lines = t_count * SLAB
        n0 = pl.multiple_of(n * 256, 256)
        g_occ = lax.dot_general(
            scaled[:lines, :N_OCC], own[pl.ds(n0, 256), :N_OCC], NT, preferred_element_type=F32)
        g_virt = lax.dot_general(
            scaled[:lines, N_OCC:], own[pl.ds(n0, 256), N_OCC:N_ORB], NT, preferred_element_type=F32)
        resp[:lines, pl.ds(n0, 256)] = (-(g_occ * g_virt)).astype(BF16)

    def apply(slot, t_first, t_count):
        lines = t_count * SLAB
        part = jnp.dot(resp[:lines], own[:, N_ORB:], preferred_element_type=F32)
        rows = pl.ds(pl.multiple_of(slot * SLAB, CHUNK), SLAB)
        applied[pl.ds(t_first, t_count), rows, :] = part.reshape(t_count, SLAB, N_POT)

    got_c = [to(far.at[B, rows_of(k)], far.at[C, rows_of(k)], z_in) for k in range(CHUNKS)]
    up_slot = jnp.where((y + 2) % 4 < 2, OWN, A)
    got_relay = to(far.at[up_slot, rows_of(2)], relay, y_up)
    down_slot = jnp.where((y + 3) % 4 < 2, B, C)
    got_d = [to(far.at[down_slot, rows_of(k)], far.at[D, rows_of(k)], y_down) for k in range(2)]
    got_d.append(to(relay, far.at[D, rows_of(2)], y_up))

    def pass_c(k):
        got_b[k].wait_recv()
        got_c[k].start()

    def pass_d(k):
        got_c[k].wait_recv()
        got_d[k].start()

    pass_c(0)
    got_a[2].wait_recv()
    got_relay.start()
    half = TIMES // 2
    t_mine, t_other = z_lo * half, (1 - z_lo) * half

    def half_tile(n, carry):
        @pl.when(n == 1)
        def _():
            got_relay.wait_recv()
            got_d[2].start()
            pass_d(0)
        tile(n, half)
        return carry

    def full_tile(slot, column, carry):
        @pl.when((slot == OWN) & (column == 1))
        def _():
            got_own.wait_recv()

        @pl.when((slot == B) & (column == 1))
        def _():
            pass_d(1)

        tile(column, TIMES)
        return carry

    def step(slot, carry):
        @pl.when(slot == B)
        def _():
            pass_c(1)
            got_a[1].wait_recv()
            got_a[0].wait_recv()
            scale(A, t_mine, half)
            lax.fori_loop(0, 3, half_tile, 0)
            apply(A, t_mine, half)
            applied[pl.ds(t_other, half), A * SLAB:(A + 1) * SLAB, :] = jnp.zeros((half, SLAB, N_POT), F32)
            pass_c(2)

        @pl.when(slot == C)
        def _():
            got_c[2].wait_recv()

        @pl.when(slot == D)
        def _():
            for k in (2, 0, 1):
                got_d[k].wait_recv()

        scale(slot, 0, TIMES)
        lax.fori_loop(0, 3, functools.partial(full_tile, slot), 0)
        apply(slot, 0, TIMES)
        return carry

    lax.fori_loop(0, 4, step, 0)

    pot_far[0:SLAB] = far[OWN, :, N_ORB:] * jnp.asarray(0.5, BF16)
    for slot in (B, C, D, A):
        pot_far[slot * SLAB:(slot + 1) * SLAB] = far[slot, :, N_ORB:]
    used = 5 * SLAB
    pot_far[used:] = jnp.zeros((N_POT - used, N_POT), BF16)
    pot_t = pot_far[...].T
    applied[:, used:, :] = jnp.zeros((TIMES, N_POT - used, N_POT), F32)

    def project(t, carry):
        whole = applied[t]
        high = whole.astype(BF16)
        low = (whole - high.astype(F32)).astype(BF16)
        both = jnp.dot(pot_t, high, preferred_element_type=F32) + jnp.dot(
            pot_t, low, preferred_element_type=F32)
        proj[t, 0:128] = both[:128, :128]
        proj[t, 128:256] = both[:128, 128:] + both[128:, :128].T
        proj[t, 256:384] = both[128:, 128:]
        return carry

    lax.fori_loop(0, TIMES, project, 0, unroll=8)

    def combine(h, a, w, carry):
        w_zh, w_x = w // 4, w % 4
        weight = [tw_all[t, pl.ds(w, 1), :] for t in range(TIMES)]
        for zl in range(2):
            for yy in range(4):
                rows = pl.ds(pl.multiple_of(((h * 3 + a) * 8 + zl * 4 + yy) * 8, 8), 8)
                total = weight[0] * proj[0, rows]
                for t in range(1, TIMES):
                    total = total + weight[t] * proj[t, rows]
                zz = w_zh * 2 + zl
                spot = ((w_x, yy, zz), (yy, zz, w_x), (zz, w_x, yy))[a]
                sums[h, a, spot[0], spot[1], spot[2]] = total
        return carry

    swaps = []
    for a in range(3):
        lax.fori_loop(0, TIMES, functools.partial(combine, 1 - core, a), 0, unroll=2)
        swap = pltpu.make_async_remote_copy(
            src_ref=sums.at[1 - core, a], dst_ref=from_core.at[a],
            send_sem=core_sem.at[a], recv_sem=core_sem.at[3 + a],
            device_id=sibling, device_id_type=MESH)
        swap.start()
        swaps.append(swap)
    copies = []
    wave = []
    for a in range(3):
        lax.fori_loop(0, TIMES, functools.partial(combine, core, a), 0, unroll=2)
        swaps[a].wait_recv()
        from_core[a] = from_core[a] + sums[core, a]
        sends = []
        for d in (2, 1, 3):
            i = a * 3 + d - 1
            copy = pltpu.make_async_remote_copy(
                src_ref=from_core.at[a, ahead[a][d]], dst_ref=arrive1.at[a, d - 1],
                send_sem=ring_send.at[i], recv_sem=ring_recv.at[i],
                device_id=off(*[d if k == a else 0 for k in range(3)]), device_id_type=MESH)
            copy.start()
            sends.append(copy)
        wave.append(sends)
        copies += sends
    for copy in sent + tw_copies:
        copy.wait_send()
    planes = []
    for a in range(3):
        for copy in wave[a]:
            copy.wait_recv()
        left1[a] = from_core[a, place[a]] + arrive1[a, 0] + arrive1[a, 1] + arrive1[a, 2]

        second, third = (a + 1) % 3, (a + 2) % 3
        for d in range(1, 16):
            steps = [0] * 3
            steps[second], steps[third] = d // 4, d % 4
            pltpu.make_async_remote_copy(
                src_ref=left1.at[a, ahead[second][d // 4], ahead[third][d % 4]], dst_ref=arrive2.at[a, d - 1],
                send_sem=plane_sem.at[a], recv_sem=plane_sem.at[3 + a],
                device_id=off(*steps), device_id_type=MESH).start()
        planes.append(pltpu.make_async_remote_copy(
            src_ref=arrive2.at[a], dst_ref=arrive2.at[a], send_sem=plane_sem.at[a],
            recv_sem=plane_sem.at[3 + a], device_id=sibling, device_id_type=MESH))
    for a in range(3):
        planes[a].wait_recv()
        total = left1[a, place[(a + 1) % 3], place[(a + 2) % 3]]
        for d in range(15):
            total = total + arrive2[a, d]
        final[a] = total

    def spread(i, src, dst, peer):
        copy = pltpu.make_async_remote_copy(
            src_ref=src, dst_ref=dst, send_sem=all_send.at[i], recv_sem=all_recv.at[i],
            device_id=peer, device_id_type=MESH)
        copy.start()
        return copy

    corner = z_lo * 4 + y
    wide = []
    for i in range(15):
        d, other = (i + 1) % 8, (i + 1) // 8
        peer = at(z_lo_=lax.rem(z_lo + d // 4, 2), y_=ahead[1][d % 4], core_=1 - core if other else core)
        wide.append(spread(i, final, whole_out.at[core, corner], peer))
    near = []
    whole_out[core, corner] = final[...]
    for copy in swaps + copies + planes:
        copy.wait_send()
    for copy in wide:
        copy.wait_recv()
    rows = []
    for h in range(2):
        for a in range(3):
            for zl in range(2):
                for yy in range(4):
                    rows.append(whole_out[h, zl * 4 + yy, a])
    low, mid, high = [jnp.concatenate(rows[16 * b:16 * b + 16], axis=0) for b in range(3)]
    out_ref[0, :128, :128] = low + low.T
    out_ref[0, :128, 128:] = mid
    out_ref[0, 128:, :128] = mid.T
    out_ref[0, 128:, 128:] = high + high.T
    for copy in wide:
        copy.wait_send()


def body(occ, virt, pot, occ_energy, virt_energy, times, weights):
    anywhere, vmem = pl.BlockSpec(memory_space=pl.ANY), pl.BlockSpec(memory_space=pltpu.VMEM)
    smem = pl.BlockSpec(memory_space=pltpu.SMEM)
    return pl.pallas_call(
        kernel,
        out_shape=jax.ShapeDtypeStruct((1, N_POT, N_POT), F32),
        in_specs=[anywhere] * 3 + [vmem] * 2 + [smem] * 2,
        out_specs=vmem,
        scratch_shapes=[
            pltpu.VMEM((2 * ROWS, WIDTH), BF16),
            pltpu.VMEM((5, SLAB, WIDTH), BF16),
            pltpu.VMEM((CHUNK, WIDTH), BF16),
            pltpu.VMEM((TIMES * SLAB, N_ORB), BF16),
            pltpu.VMEM((TIMES * SLAB, 2 * ROWS), BF16),
            pltpu.VMEM((TIMES, N_POT, N_POT), F32),
            pltpu.VMEM((TIMES, 1, N_ORB), F32),
            pltpu.VMEM((TIMES, 16, 128), F32),
            pltpu.VMEM((N_POT, N_POT), BF16),
            pltpu.VMEM((TIMES, 384, 128), F32),
            pltpu.VMEM((2, 3, 4, 4, 4, 8, 128), F32),
            pltpu.VMEM((3, 4, 4, 4, 8, 128), F32),
            pltpu.VMEM((3, 3, 4, 4, 8, 128), F32),
            pltpu.VMEM((3, 15, 8, 128), F32),
            pltpu.VMEM((3, 4, 4, 8, 128), F32),
            pltpu.VMEM((3, 8, 128), F32),
            pltpu.VMEM((2, 8, 3, 8, 128), F32),
            pltpu.SemaphoreType.DMA((6,)),
            pltpu.SemaphoreType.DMA((24,)),
            pltpu.SemaphoreType.DMA((24,)),
            pltpu.SemaphoreType.DMA((7,)),
            pltpu.SemaphoreType.DMA((7,)),
            pltpu.SemaphoreType.DMA((6,)),
            pltpu.SemaphoreType.DMA((9,)),
            pltpu.SemaphoreType.DMA((9,)),
            pltpu.SemaphoreType.DMA((6,)),
            pltpu.SemaphoreType.DMA((15,)),
            pltpu.SemaphoreType.DMA((15,)),
        ],
        compiler_params=pltpu.CompilerParams(
            collective_id=0, has_side_effects=True, vmem_limit_bytes=60 * 2**20),
    )(occ, virt, pot, occ_energy[None, :], virt_energy[None, :], times, weights.T)


def solution(mesh):
    return jax.shard_map(
        body,
        mesh=mesh,
        in_specs=(P("pts", None), P("pts", None), P("pts", None), P(), P(), P("tau"), P(None, "tau")),
        out_specs=P("tau", None, None),
        check_vma=False,
    )
```

```python
import functools

import jax
import jax.numpy as jnp
from jax import lax
from jax.experimental import pallas as pl
from jax.experimental.pallas import tpu as pltpu
from jax.sharding import PartitionSpec as P

MESH = pl.DeviceIdType.MESH
NT = (((1,), (1,)), ((), ()))
N_OCC, N_VIRT, N_POT, ROWS = 2048, 4096, 256, 384
N_ORB = N_OCC + N_VIRT
WIDTH = N_ORB + N_POT
TIMES = 8
SLAB = ROWS // TIMES
CHUNK = 16
CHUNKS = SLAB // CHUNK
OWN, B, C, D, A = range(5)
F32, BF16 = jnp.float32, jnp.bfloat16


def kernel(
    occ_ref, virt_ref, pot_ref, occ_e_ref, virt_e_ref, times_ref, weights_ref, out_ref,
    own, far, relay, scaled, resp, applied, factor, tw_all, pot_far, proj,
    sums, from_core, arrive1, arrive2, left1, final, whole_out,
    load_sem, send_sem, recv_sem, tw_send, tw_recv,
    core_sem, ring_send, ring_recv, plane_sem, all_send, all_recv,
):
    pts, tau = lax.axis_index("pts"), lax.axis_index("tau")
    z_lo, y, core = pts // 8, (pts // 2) % 4, pts % 2
    z_hi, x = tau // 4, tau % 4

    def at(z_lo_=None, y_=None, core_=None, z_hi_=None):
        zl = z_lo if z_lo_ is None else z_lo_
        yy = y if y_ is None else y_
        cc = core if core_ is None else core_
        zh = z_hi if z_hi_ is None else z_hi_
        return (zl * 8 + yy * 2 + cc, zh * 4 + x)

    sibling = at(core_=1 - core)
    z_out = at(z_lo_=1 - z_lo, z_hi_=1 - z_hi)
    z_in = at(z_lo_=1 - z_lo)
    y_down = at(y_=(y + 3) % 4)
    y_up = at(y_=(y + 1) % 4)
    tau_peers = [
        (pts, ((z_hi + dz) % 2) * 4 + (x + dx) % 4)
        for dz, dx in ((1, 2), (1, 1), (1, 3), (1, 0), (0, 2), (0, 1), (0, 3))]
    place = (x, y, z_hi * 2 + z_lo)

    ahead = [[lax.rem(p + d, 4) for d in range(4)] for p in place]
    in_pts = [[0] * 4, [2 * c + core for c in ahead[1]], [8 * lax.rem(c, 2) for c in ahead[2]]]
    in_tau = [ahead[0], [0] * 4, [4 * lax.div(c, 2) for c in ahead[2]]]

    def off(*steps):
        return (in_pts[1][steps[1]] + in_pts[2][steps[2]], in_tau[0][steps[0]] + in_tau[2][steps[2]])

    in_planes = [
        off(i // 16, i // 4 % 4, i % 4) for i in range(1, 64) if 0 in (i // 16, i // 4 % 4, i % 4)]

    first = pl.multiple_of(tau * SLAB, CHUNK)
    parts = ((occ_ref, 0, N_OCC), (virt_ref, N_OCC, N_VIRT), (pot_ref, N_ORB, N_POT))
    loads = []
    for i, (ref, at_col, cols) in enumerate(parts):
        loads.append(pltpu.make_async_copy(
            ref.at[pl.ds(first, SLAB)], far.at[OWN, :, pl.ds(at_col, cols)], load_sem.at[i]))
    for i, (ref, at_col, cols) in enumerate(parts):
        loads.append(pltpu.make_async_copy(
            ref, own.at[pl.ds(0, ROWS), pl.ds(at_col, cols)], load_sem.at[3 + i]))
    for load in loads:
        load.start()

    barrier = pltpu.get_barrier_semaphore()
    across = [at(z_lo_=lax.rem(z_lo + d // 4, 2), y_=ahead[1][d % 4], core_=1 - core) for d in range(1, 8)]
    greeted = [sibling] + in_planes + across
    for peer in greeted:
        pl.semaphore_signal(barrier, 1, device_id=peer, device_id_type=MESH)
    for w in range(TIMES):
        tw_all[tau, w:w + 1] = jnp.full((1, 128), weights_ref[0, w], F32)
    tw_all[tau, 8:16] = jnp.full((8, 128), times_ref[0], F32)
    pl.semaphore_wait(barrier, len(greeted))

    count = iter(range(64))
    sent = []

    def to(src, dst, peer):
        i = next(count)
        copy = pltpu.make_async_remote_copy(
            src_ref=src, dst_ref=dst, send_sem=send_sem.at[i], recv_sem=recv_sem.at[i],
            device_id=peer, device_id_type=MESH)
        sent.append(copy)
        return copy

    def send(src, dst, peer):
        copy = to(src, dst, peer)
        copy.start()
        return copy

    tw_copies = []
    for i, peer in enumerate(tau_peers):
        copy = pltpu.make_async_remote_copy(
            src_ref=tw_all.at[tau], dst_ref=tw_all.at[tau], send_sem=tw_send.at[i], recv_sem=tw_recv.at[i],
            device_id=peer, device_id_type=MESH)
        copy.start()
        tw_copies.append(copy)

    def rows_of(k):
        return pl.ds(k * CHUNK, CHUNK)

    for load in loads[:3]:
        load.wait()
    got_b = [send(far.at[OWN, rows_of(k)], far.at[B, rows_of(k)], y_down) for k in range(CHUNKS)]
    for load in loads[3:]:
        load.wait()
    out_first = ((1 - z_hi) * 4 + x) * SLAB

    def own_rows(start, k):
        return own.at[pl.ds(pl.multiple_of(start + k * CHUNK, CHUNK), CHUNK)]

    got_a = {
        2: send(own_rows(first, 2), far.at[A, rows_of(2)], z_in),
        1: send(own_rows(out_first, 1), far.at[A, rows_of(1)], z_out),
        0: send(own_rows(out_first, 0), far.at[A, rows_of(0)], z_out),
    }
    got_own = send(own.at[pl.ds(0, ROWS)], own.at[pl.ds(ROWS, ROWS)], sibling)

    for copy in tw_copies:
        copy.wait_recv()
    for t in range(TIMES):
        moment = tw_all[t, 8:9, 0:1]
        factor[t, :, :N_OCC] = jnp.exp(moment * occ_e_ref[...])
        factor[t, :, N_OCC:] = jnp.exp(-moment * virt_e_ref[...])

    def scale_chunks(slot, k_first, k_end):
        def one(i, carry):
            k, t = i // TIMES, i % TIMES
            rows = pl.ds(pl.multiple_of(k * CHUNK, CHUNK), CHUNK)
            wide = far[slot, rows, pl.ds(0, N_ORB)].astype(F32) * factor[t]
            scaled[pl.ds(pl.multiple_of(t * SLAB + k * CHUNK, CHUNK), CHUNK)] = wide.astype(BF16)
            return carry
        lax.fori_loop(k_first * TIMES, k_end * TIMES, one, 0)

    def scale(slot, t_first, t_count):
        def one(i, carry):
            rows = pl.ds(pl.multiple_of((i % CHUNKS) * CHUNK, CHUNK), CHUNK)
            wide = far[slot, rows, pl.ds(0, N_ORB)].astype(F32) * factor[t_first + i // CHUNKS]
            scaled[pl.ds(pl.multiple_of(i * CHUNK, CHUNK), CHUNK)] = wide.astype(BF16)
            return carry
        lax.fori_loop(0, t_count * CHUNKS, one, 0)

    def tile(n, t_count):
        lines = t_count * SLAB
        n0 = pl.multiple_of(n * 256, 256)
        g_occ = lax.dot_general(
            scaled[:lines, :N_OCC], own[pl.ds(n0, 256), :N_OCC], NT, preferred_element_type=F32)
        g_virt = lax.dot_general(
            scaled[:lines, N_OCC:], own[pl.ds(n0, 256), N_OCC:N_ORB], NT, preferred_element_type=F32)
        resp[:lines, pl.ds(n0, 256)] = (-(g_occ * g_virt)).astype(BF16)

    def apply(slot, t_first, t_count):
        lines = t_count * SLAB
        part = jnp.dot(resp[:lines], own[:, N_ORB:], preferred_element_type=F32)
        rows = pl.ds(pl.multiple_of(slot * SLAB, CHUNK), SLAB)
        applied[pl.ds(t_first, t_count), rows, :] = part.reshape(t_count, SLAB, N_POT)

    got_c = [to(far.at[B, rows_of(k)], far.at[C, rows_of(k)], z_in) for k in range(CHUNKS)]
    up_slot = jnp.where((y + 2) % 4 < 2, OWN, A)
    got_relay = to(far.at[up_slot, rows_of(2)], relay, y_up)
    down_slot = jnp.where((y + 3) % 4 < 2, B, C)
    got_d = [to(far.at[down_slot, rows_of(k)], far.at[D, rows_of(k)], y_down) for k in range(2)]
    got_d.append(to(relay, far.at[D, rows_of(2)], y_up))

    def pass_c(k):
        got_b[k].wait_recv()
        got_c[k].start()

    def pass_d(k):
        got_c[k].wait_recv()
        got_d[k].start()

    pass_c(0)
    got_a[2].wait_recv()
    got_relay.start()
    half = TIMES // 2
    t_mine, t_other = z_lo * half, (1 - z_lo) * half

    def half_tile(n, carry):
        @pl.when(n == 1)
        def _():
            got_relay.wait_recv()
            got_d[2].start()
            pass_d(0)
        tile(n, half)
        return carry

    def full_tile(slot, column, carry):
        @pl.when((slot == OWN) & (column == 1))
        def _():
            got_own.wait_recv()

        @pl.when((slot == B) & (column == 1))
        def _():
            pass_d(1)

        tile(column, TIMES)
        return carry

    def step(slot, carry):
        @pl.when(slot == B)
        def _():
            pass_c(1)
            got_a[1].wait_recv()
            got_a[0].wait_recv()
            scale(A, t_mine, half)
            lax.fori_loop(0, 3, half_tile, 0)
            apply(A, t_mine, half)
            applied[pl.ds(t_other, half), A * SLAB:(A + 1) * SLAB, :] = jnp.zeros((half, SLAB, N_POT), F32)

        @pl.when(slot == D)
        def _():
            for k in (2, 0, 1):
                got_d[k].wait_recv()


        scale_chunks(slot, 0, 2)

        @pl.when(slot == B)
        def _():
            pass_c(2)

        @pl.when(slot == C)
        def _():
            got_c[2].wait_recv()

        scale_chunks(slot, 2, CHUNKS)
        lax.fori_loop(0, 3, functools.partial(full_tile, slot), 0)
        apply(slot, 0, TIMES)
        return carry

    lax.fori_loop(0, 4, step, 0)

    pot_far[0:SLAB] = far[OWN, :, N_ORB:] * jnp.asarray(0.5, BF16)
    for slot in (B, C, D, A):
        pot_far[slot * SLAB:(slot + 1) * SLAB] = far[slot, :, N_ORB:]
    used = 5 * SLAB
    pot_far[used:] = jnp.zeros((N_POT - used, N_POT), BF16)
    pot_t = pot_far[...].T
    applied[:, used:, :] = jnp.zeros((TIMES, N_POT - used, N_POT), F32)

    def project(t, carry):
        whole = applied[t]
        high = whole.astype(BF16)
        low = (whole - high.astype(F32)).astype(BF16)
        both = jnp.dot(pot_t, high, preferred_element_type=F32) + jnp.dot(
            pot_t, low, preferred_element_type=F32)
        proj[t, 0:128] = both[:128, :128]
        proj[t, 128:256] = both[:128, 128:] + both[128:, :128].T
        proj[t, 256:384] = both[128:, 128:]
        return carry

    lax.fori_loop(0, TIMES, project, 0, unroll=8)

    def combine(h, a, w, carry):
        w_zh, w_x = w // 4, w % 4
        weight = [tw_all[t, pl.ds(w, 1), :] for t in range(TIMES)]
        for zl in range(2):
            for yy in range(4):
                rows = pl.ds(pl.multiple_of(((h * 3 + a) * 8 + zl * 4 + yy) * 8, 8), 8)
                total = weight[0] * proj[0, rows]
                for t in range(1, TIMES):
                    total = total + weight[t] * proj[t, rows]
                zz = w_zh * 2 + zl
                spot = ((w_x, yy, zz), (yy, zz, w_x), (zz, w_x, yy))[a]
                sums[h, a, spot[0], spot[1], spot[2]] = total
        return carry

    swaps = []
    for a in range(3):
        lax.fori_loop(0, TIMES, functools.partial(combine, 1 - core, a), 0, unroll=2)
        swap = pltpu.make_async_remote_copy(
            src_ref=sums.at[1 - core, a], dst_ref=from_core.at[a],
            send_sem=core_sem.at[a], recv_sem=core_sem.at[3 + a],
            device_id=sibling, device_id_type=MESH)
        swap.start()
        swaps.append(swap)
    copies = []
    wave = []
    for a in range(3):
        lax.fori_loop(0, TIMES, functools.partial(combine, core, a), 0, unroll=2)
        swaps[a].wait_recv()
        from_core[a] = from_core[a] + sums[core, a]
        sends = []
        for d in (2, 1, 3):
            i = a * 3 + d - 1
            copy = pltpu.make_async_remote_copy(
                src_ref=from_core.at[a, ahead[a][d]], dst_ref=arrive1.at[a, d - 1],
                send_sem=ring_send.at[i], recv_sem=ring_recv.at[i],
                device_id=off(*[d if k == a else 0 for k in range(3)]), device_id_type=MESH)
            copy.start()
            sends.append(copy)
        wave.append(sends)
        copies += sends
    for copy in sent + tw_copies:
        copy.wait_send()
    planes = []
    for a in range(3):
        for copy in wave[a]:
            copy.wait_recv()
        left1[a] = from_core[a, place[a]] + arrive1[a, 0] + arrive1[a, 1] + arrive1[a, 2]

        second, third = (a + 1) % 3, (a + 2) % 3
        for d in range(1, 16):
            steps = [0] * 3
            steps[second], steps[third] = d // 4, d % 4
            pltpu.make_async_remote_copy(
                src_ref=left1.at[a, ahead[second][d // 4], ahead[third][d % 4]], dst_ref=arrive2.at[a, d - 1],
                send_sem=plane_sem.at[a], recv_sem=plane_sem.at[3 + a],
                device_id=off(*steps), device_id_type=MESH).start()
        planes.append(pltpu.make_async_remote_copy(
            src_ref=arrive2.at[a], dst_ref=arrive2.at[a], send_sem=plane_sem.at[a],
            recv_sem=plane_sem.at[3 + a], device_id=sibling, device_id_type=MESH))
    for a in range(3):
        planes[a].wait_recv()
        total = left1[a, place[(a + 1) % 3], place[(a + 2) % 3]]
        for d in range(15):
            total = total + arrive2[a, d]
        final[a] = total

    def spread(i, src, dst, peer):
        copy = pltpu.make_async_remote_copy(
            src_ref=src, dst_ref=dst, send_sem=all_send.at[i], recv_sem=all_recv.at[i],
            device_id=peer, device_id_type=MESH)
        copy.start()
        return copy

    corner = z_lo * 4 + y
    wide = []
    for i in range(15):
        d, other = (i + 1) % 8, (i + 1) // 8
        peer = at(z_lo_=lax.rem(z_lo + d // 4, 2), y_=ahead[1][d % 4], core_=1 - core if other else core)
        wide.append(spread(i, final, whole_out.at[core, corner], peer))
    near = []
    whole_out[core, corner] = final[...]
    for copy in swaps + copies + planes:
        copy.wait_send()
    for copy in wide:
        copy.wait_recv()
    rows = []
    for h in range(2):
        for a in range(3):
            for zl in range(2):
                for yy in range(4):
                    rows.append(whole_out[h, zl * 4 + yy, a])
    low, mid, high = [jnp.concatenate(rows[16 * b:16 * b + 16], axis=0) for b in range(3)]
    out_ref[0, :128, :128] = low + low.T
    out_ref[0, :128, 128:] = mid
    out_ref[0, 128:, :128] = mid.T
    out_ref[0, 128:, 128:] = high + high.T
    for copy in wide:
        copy.wait_send()


def body(occ, virt, pot, occ_energy, virt_energy, times, weights):
    anywhere, vmem = pl.BlockSpec(memory_space=pl.ANY), pl.BlockSpec(memory_space=pltpu.VMEM)
    smem = pl.BlockSpec(memory_space=pltpu.SMEM)
    return pl.pallas_call(
        kernel,
        out_shape=jax.ShapeDtypeStruct((1, N_POT, N_POT), F32),
        in_specs=[anywhere] * 3 + [vmem] * 2 + [smem] * 2,
        out_specs=vmem,
        scratch_shapes=[
            pltpu.VMEM((2 * ROWS, WIDTH), BF16),
            pltpu.VMEM((5, SLAB, WIDTH), BF16),
            pltpu.VMEM((CHUNK, WIDTH), BF16),
            pltpu.VMEM((TIMES * SLAB, N_ORB), BF16),
            pltpu.VMEM((TIMES * SLAB, 2 * ROWS), BF16),
            pltpu.VMEM((TIMES, N_POT, N_POT), F32),
            pltpu.VMEM((TIMES, 1, N_ORB), F32),
            pltpu.VMEM((TIMES, 16, 128), F32),
            pltpu.VMEM((N_POT, N_POT), BF16),
            pltpu.VMEM((TIMES, 384, 128), F32),
            pltpu.VMEM((2, 3, 4, 4, 4, 8, 128), F32),
            pltpu.VMEM((3, 4, 4, 4, 8, 128), F32),
            pltpu.VMEM((3, 3, 4, 4, 8, 128), F32),
            pltpu.VMEM((3, 15, 8, 128), F32),
            pltpu.VMEM((3, 4, 4, 8, 128), F32),
            pltpu.VMEM((3, 8, 128), F32),
            pltpu.VMEM((2, 8, 3, 8, 128), F32),
            pltpu.SemaphoreType.DMA((6,)),
            pltpu.SemaphoreType.DMA((24,)),
            pltpu.SemaphoreType.DMA((24,)),
            pltpu.SemaphoreType.DMA((7,)),
            pltpu.SemaphoreType.DMA((7,)),
            pltpu.SemaphoreType.DMA((6,)),
            pltpu.SemaphoreType.DMA((9,)),
            pltpu.SemaphoreType.DMA((9,)),
            pltpu.SemaphoreType.DMA((6,)),
            pltpu.SemaphoreType.DMA((15,)),
            pltpu.SemaphoreType.DMA((15,)),
        ],
        compiler_params=pltpu.CompilerParams(
            collective_id=0, has_side_effects=True, vmem_limit_bytes=60 * 2**20),
    )(occ, virt, pot, occ_energy[None, :], virt_energy[None, :], times, weights.T)


def solution(mesh):
    return jax.shard_map(
        body,
        mesh=mesh,
        in_specs=(P("pts", None), P("pts", None), P("pts", None), P(), P(), P("tau"), P(None, "tau")),
        out_specs=P("tau", None, None),
        check_vma=False,
    )
```

```python
import functools

import jax
import jax.numpy as jnp
from jax import lax
from jax.experimental import pallas as pl
from jax.experimental.pallas import tpu as pltpu
from jax.sharding import PartitionSpec as P

MESH = pl.DeviceIdType.MESH
NT = (((1,), (1,)), ((), ()))
N_OCC, N_VIRT, N_POT, ROWS = 2048, 4096, 256, 384
N_ORB = N_OCC + N_VIRT
WIDTH = N_ORB + N_POT
TIMES = 8
SLAB = ROWS // TIMES
CHUNK = 16
CHUNKS = SLAB // CHUNK
OWN, B, C, D, A = range(5)
F32, BF16 = jnp.float32, jnp.bfloat16


def kernel(
    occ_ref, virt_ref, pot_ref, occ_e_ref, virt_e_ref, times_ref, weights_ref, out_ref,
    own, far, relay, scaled, resp, applied, factor, tw_all, pot_far, proj,
    sums, from_core, arrive1, arrive2, left1, final, whole_out,
    load_sem, send_sem, recv_sem, tw_send, tw_recv,
    core_sem, ring_send, ring_recv, plane_sem, all_send, all_recv,
):
    pts, tau = lax.axis_index("pts"), lax.axis_index("tau")
    z_lo, y, core = pts // 8, (pts // 2) % 4, pts % 2
    z_hi, x = tau // 4, tau % 4

    def at(z_lo_=None, y_=None, core_=None, z_hi_=None):
        zl = z_lo if z_lo_ is None else z_lo_
        yy = y if y_ is None else y_
        cc = core if core_ is None else core_
        zh = z_hi if z_hi_ is None else z_hi_
        return (zl * 8 + yy * 2 + cc, zh * 4 + x)

    sibling = at(core_=1 - core)
    z_out = at(z_lo_=1 - z_lo, z_hi_=1 - z_hi)
    z_in = at(z_lo_=1 - z_lo)
    y_down = at(y_=(y + 3) % 4)
    y_up = at(y_=(y + 1) % 4)
    tau_peers = [
        (pts, ((z_hi + dz) % 2) * 4 + (x + dx) % 4)
        for dz, dx in ((1, 2), (1, 1), (1, 3), (1, 0), (0, 2), (0, 1), (0, 3))]
    place = (x, y, z_hi * 2 + z_lo)

    ahead = [[lax.rem(p + d, 4) for d in range(4)] for p in place]
    in_pts = [[0] * 4, [2 * c + core for c in ahead[1]], [8 * lax.rem(c, 2) for c in ahead[2]]]
    in_tau = [ahead[0], [0] * 4, [4 * lax.div(c, 2) for c in ahead[2]]]

    def off(*steps):
        return (in_pts[1][steps[1]] + in_pts[2][steps[2]], in_tau[0][steps[0]] + in_tau[2][steps[2]])

    in_planes = [
        off(i // 16, i // 4 % 4, i % 4) for i in range(1, 64) if 0 in (i // 16, i // 4 % 4, i % 4)]

    first = pl.multiple_of(tau * SLAB, CHUNK)
    parts = ((occ_ref, 0, N_OCC), (virt_ref, N_OCC, N_VIRT), (pot_ref, N_ORB, N_POT))
    loads = []
    for i, (ref, at_col, cols) in enumerate(parts):
        loads.append(pltpu.make_async_copy(
            ref.at[pl.ds(first, SLAB)], far.at[OWN, :, pl.ds(at_col, cols)], load_sem.at[i]))
    for i, (ref, at_col, cols) in enumerate(parts):
        loads.append(pltpu.make_async_copy(
            ref, own.at[pl.ds(0, ROWS), pl.ds(at_col, cols)], load_sem.at[3 + i]))
    for load in loads:
        load.start()

    barrier = pltpu.get_barrier_semaphore()
    across = [at(z_lo_=lax.rem(z_lo + d // 4, 2), y_=ahead[1][d % 4], core_=1 - core) for d in range(1, 8)]
    greeted = [sibling] + in_planes + across
    for peer in greeted:
        pl.semaphore_signal(barrier, 1, device_id=peer, device_id_type=MESH)
    for w in range(TIMES):
        tw_all[tau, w:w + 1] = jnp.full((1, 128), weights_ref[0, w], F32)
    tw_all[tau, 8:16] = jnp.full((8, 128), times_ref[0], F32)
    pl.semaphore_wait(barrier, len(greeted))

    count = iter(range(64))
    sent = []

    def to(src, dst, peer):
        i = next(count)
        copy = pltpu.make_async_remote_copy(
            src_ref=src, dst_ref=dst, send_sem=send_sem.at[i], recv_sem=recv_sem.at[i],
            device_id=peer, device_id_type=MESH)
        sent.append(copy)
        return copy

    def send(src, dst, peer):
        copy = to(src, dst, peer)
        copy.start()
        return copy

    tw_copies = []
    for i, peer in enumerate(tau_peers):
        copy = pltpu.make_async_remote_copy(
            src_ref=tw_all.at[tau], dst_ref=tw_all.at[tau], send_sem=tw_send.at[i], recv_sem=tw_recv.at[i],
            device_id=peer, device_id_type=MESH)
        copy.start()
        tw_copies.append(copy)

    def rows_of(k):
        return pl.ds(k * CHUNK, CHUNK)

    for load in loads[:3]:
        load.wait()
    got_b = [send(far.at[OWN, rows_of(k)], far.at[B, rows_of(k)], y_down) for k in range(CHUNKS)]
    for load in loads[3:]:
        load.wait()
    out_first = ((1 - z_hi) * 4 + x) * SLAB

    def own_rows(start, k):
        return own.at[pl.ds(pl.multiple_of(start + k * CHUNK, CHUNK), CHUNK)]

    got_a = {
        2: send(own_rows(first, 2), far.at[A, rows_of(2)], z_in),
        1: send(own_rows(out_first, 1), far.at[A, rows_of(1)], z_out),
        0: send(own_rows(out_first, 0), far.at[A, rows_of(0)], z_out),
    }
    got_own = send(own.at[pl.ds(0, ROWS)], own.at[pl.ds(ROWS, ROWS)], sibling)

    pot_far[0:SLAB] = far[OWN, :, N_ORB:] * jnp.asarray(0.5, BF16)
    used = 5 * SLAB
    pot_far[used:] = jnp.zeros((N_POT - used, N_POT), BF16)
    applied[:, used:, :] = jnp.zeros((TIMES, N_POT - used, N_POT), F32)
    for copy in tw_copies:
        copy.wait_recv()
    for t in range(TIMES):
        moment = tw_all[t, 8:9, 0:1]
        factor[t, :, :N_OCC] = jnp.exp(moment * occ_e_ref[...])
        factor[t, :, N_OCC:] = jnp.exp(-moment * virt_e_ref[...])

    def scale_chunks(slot, k_first, k_end):
        pieces, span = 6, N_ORB // 6

        def one(i, carry):
            k = i // pieces
            lanes = pl.ds(pl.multiple_of((i % pieces) * span, 128), span)
            wide = far[slot, pl.ds(pl.multiple_of(k * CHUNK, CHUNK), CHUNK), lanes].astype(F32)
            for t in range(TIMES):
                rows = pl.ds(pl.multiple_of(t * SLAB + k * CHUNK, CHUNK), CHUNK)
                scaled[rows, lanes] = (wide * factor[t, :, lanes]).astype(BF16)
            return carry
        lax.fori_loop(k_first * pieces, k_end * pieces, one, 0)

    def scale(slot, t_first, t_count):
        def one(i, carry):
            rows = pl.ds(pl.multiple_of((i % CHUNKS) * CHUNK, CHUNK), CHUNK)
            wide = far[slot, rows, pl.ds(0, N_ORB)].astype(F32) * factor[t_first + i // CHUNKS]
            scaled[pl.ds(pl.multiple_of(i * CHUNK, CHUNK), CHUNK)] = wide.astype(BF16)
            return carry
        lax.fori_loop(0, t_count * CHUNKS, one, 0)

    def tile(n, t_count):
        lines = t_count * SLAB
        n0 = pl.multiple_of(n * 256, 256)
        g_occ = lax.dot_general(
            scaled[:lines, :N_OCC], own[pl.ds(n0, 256), :N_OCC], NT, preferred_element_type=F32)
        g_virt = lax.dot_general(
            scaled[:lines, N_OCC:], own[pl.ds(n0, 256), N_OCC:N_ORB], NT, preferred_element_type=F32)
        resp[:lines, pl.ds(n0, 256)] = (-(g_occ * g_virt)).astype(BF16)

    def apply(slot, t_first, t_count):
        lines = t_count * SLAB
        part = jnp.dot(resp[:lines], own[:, N_ORB:], preferred_element_type=F32)
        rows = pl.ds(pl.multiple_of(slot * SLAB, CHUNK), SLAB)
        applied[pl.ds(t_first, t_count), rows, :] = part.reshape(t_count, SLAB, N_POT)

    got_c = [to(far.at[B, rows_of(k)], far.at[C, rows_of(k)], z_in) for k in range(CHUNKS)]
    up_slot = jnp.where((y + 2) % 4 < 2, OWN, A)
    got_relay = to(far.at[up_slot, rows_of(2)], relay, y_up)
    down_slot = jnp.where((y + 3) % 4 < 2, B, C)
    got_d = [to(far.at[down_slot, rows_of(k)], far.at[D, rows_of(k)], y_down) for k in range(2)]
    got_d.append(to(relay, far.at[D, rows_of(2)], y_up))

    def pass_c(k):
        got_b[k].wait_recv()
        got_c[k].start()

    def pass_d(k):
        got_c[k].wait_recv()
        got_d[k].start()

    pass_c(0)
    got_a[2].wait_recv()
    got_relay.start()
    half = TIMES // 2
    t_mine, t_other = z_lo * half, (1 - z_lo) * half

    def half_tile(n, carry):
        @pl.when(n == 1)
        def _():
            got_relay.wait_recv()
            got_d[2].start()
            pass_d(0)
        tile(n, half)
        return carry

    def full_tile(slot, column, carry):
        @pl.when((slot == OWN) & (column == 1))
        def _():
            got_own.wait_recv()

        @pl.when((slot == B) & (column == 1))
        def _():
            pass_d(1)

        tile(column, TIMES)
        return carry

    def step(slot, carry):
        @pl.when(slot == B)
        def _():
            pass_c(1)
            got_a[1].wait_recv()
            got_a[0].wait_recv()
            scale(A, t_mine, half)
            lax.fori_loop(0, 3, half_tile, 0)
            apply(A, t_mine, half)
            applied[pl.ds(t_other, half), A * SLAB:(A + 1) * SLAB, :] = jnp.zeros((half, SLAB, N_POT), F32)

        @pl.when(slot == D)
        def _():
            for k in (2, 0, 1):
                got_d[k].wait_recv()


        scale_chunks(slot, 0, 2)

        @pl.when(slot == B)
        def _():
            pass_c(2)

        @pl.when(slot == C)
        def _():
            got_c[2].wait_recv()

        scale_chunks(slot, 2, CHUNKS)
        lax.fori_loop(0, 3, functools.partial(full_tile, slot), 0)
        apply(slot, 0, TIMES)
        return carry

    lax.fori_loop(0, 4, step, 0)

    for slot in (B, C, D, A):
        pot_far[slot * SLAB:(slot + 1) * SLAB] = far[slot, :, N_ORB:]
    pot_t = pot_far[...].T

    def project(t, carry):
        whole = applied[t]
        high = whole.astype(BF16)
        low = (whole - high.astype(F32)).astype(BF16)
        both = jnp.dot(pot_t, high, preferred_element_type=F32) + jnp.dot(
            pot_t, low, preferred_element_type=F32)
        proj[t, 0:128] = both[:128, :128]
        proj[t, 128:256] = both[:128, 128:] + both[128:, :128].T
        proj[t, 256:384] = both[128:, 128:]
        return carry

    lax.fori_loop(0, TIMES, project, 0, unroll=8)

    def combine(h, a, w, carry):
        w_zh, w_x = w // 4, w % 4
        weight = [tw_all[t, pl.ds(w, 1), :] for t in range(TIMES)]
        for zl in range(2):
            for yy in range(4):
                rows = pl.ds(pl.multiple_of(((h * 3 + a) * 8 + zl * 4 + yy) * 8, 8), 8)
                total = weight[0] * proj[0, rows]
                for t in range(1, TIMES):
                    total = total + weight[t] * proj[t, rows]
                zz = w_zh * 2 + zl
                spot = ((w_x, yy, zz), (yy, zz, w_x), (zz, w_x, yy))[a]
                sums[h, a, spot[0], spot[1], spot[2]] = total
        return carry

    swaps = []
    for a in range(3):
        lax.fori_loop(0, TIMES, functools.partial(combine, 1 - core, a), 0, unroll=4)
        swap = pltpu.make_async_remote_copy(
            src_ref=sums.at[1 - core, a], dst_ref=from_core.at[a],
            send_sem=core_sem.at[a], recv_sem=core_sem.at[3 + a],
            device_id=sibling, device_id_type=MESH)
        swap.start()
        swaps.append(swap)
    copies = []
    wave = []
    for a in range(3):
        lax.fori_loop(0, TIMES, functools.partial(combine, core, a), 0, unroll=4)
        swaps[a].wait_recv()
        from_core[a] = from_core[a] + sums[core, a]
        sends = []
        for d in (2, 1, 3):
            i = a * 3 + d - 1
            copy = pltpu.make_async_remote_copy(
                src_ref=from_core.at[a, ahead[a][d]], dst_ref=arrive1.at[a, d - 1],
                send_sem=ring_send.at[i], recv_sem=ring_recv.at[i],
                device_id=off(*[d if k == a else 0 for k in range(3)]), device_id_type=MESH)
            copy.start()
            sends.append(copy)
        wave.append(sends)
        copies += sends
    for copy in sent + tw_copies:
        copy.wait_send()
    planes = []
    for a in range(3):
        for copy in wave[a]:
            copy.wait_recv()
        left1[a] = from_core[a, place[a]] + arrive1[a, 0] + arrive1[a, 1] + arrive1[a, 2]

        second, third = (a + 1) % 3, (a + 2) % 3
        for d in range(1, 16):
            steps = [0] * 3
            steps[second], steps[third] = d // 4, d % 4
            pltpu.make_async_remote_copy(
                src_ref=left1.at[a, ahead[second][d // 4], ahead[third][d % 4]], dst_ref=arrive2.at[a, d - 1],
                send_sem=plane_sem.at[a], recv_sem=plane_sem.at[3 + a],
                device_id=off(*steps), device_id_type=MESH).start()
        planes.append(pltpu.make_async_remote_copy(
            src_ref=arrive2.at[a], dst_ref=arrive2.at[a], send_sem=plane_sem.at[a],
            recv_sem=plane_sem.at[3 + a], device_id=sibling, device_id_type=MESH))
    for a in range(3):
        planes[a].wait_recv()
        total = left1[a, place[(a + 1) % 3], place[(a + 2) % 3]]
        for d in range(15):
            total = total + arrive2[a, d]
        final[a] = total

    def spread(i, src, dst, peer):
        copy = pltpu.make_async_remote_copy(
            src_ref=src, dst_ref=dst, send_sem=all_send.at[i], recv_sem=all_recv.at[i],
            device_id=peer, device_id_type=MESH)
        copy.start()
        return copy

    corner = z_lo * 4 + y
    wide = []
    for i in range(15):
        d, other = (i + 1) % 8, (i + 1) // 8
        peer = at(z_lo_=lax.rem(z_lo + d // 4, 2), y_=ahead[1][d % 4], core_=1 - core if other else core)
        wide.append(spread(i, final, whole_out.at[core, corner], peer))
    near = []
    whole_out[core, corner] = final[...]
    for copy in swaps + copies + planes:
        copy.wait_send()
    for copy in wide:
        copy.wait_recv()
    rows = []
    for h in range(2):
        for a in range(3):
            for zl in range(2):
                for yy in range(4):
                    rows.append(whole_out[h, zl * 4 + yy, a])
    low, mid, high = [jnp.concatenate(rows[16 * b:16 * b + 16], axis=0) for b in range(3)]
    out_ref[0, :128, :128] = low + low.T
    out_ref[0, :128, 128:] = mid
    out_ref[0, 128:, :128] = mid.T
    out_ref[0, 128:, 128:] = high + high.T
    for copy in wide:
        copy.wait_send()


def body(occ, virt, pot, occ_energy, virt_energy, times, weights):
    anywhere, vmem = pl.BlockSpec(memory_space=pl.ANY), pl.BlockSpec(memory_space=pltpu.VMEM)
    smem = pl.BlockSpec(memory_space=pltpu.SMEM)
    return pl.pallas_call(
        kernel,
        out_shape=jax.ShapeDtypeStruct((1, N_POT, N_POT), F32),
        in_specs=[anywhere] * 3 + [vmem] * 2 + [smem] * 2,
        out_specs=vmem,
        scratch_shapes=[
            pltpu.VMEM((2 * ROWS, WIDTH), BF16),
            pltpu.VMEM((5, SLAB, WIDTH), BF16),
            pltpu.VMEM((CHUNK, WIDTH), BF16),
            pltpu.VMEM((TIMES * SLAB, N_ORB), BF16),
            pltpu.VMEM((TIMES * SLAB, 2 * ROWS), BF16),
            pltpu.VMEM((TIMES, N_POT, N_POT), F32),
            pltpu.VMEM((TIMES, 1, N_ORB), F32),
            pltpu.VMEM((TIMES, 16, 128), F32),
            pltpu.VMEM((N_POT, N_POT), BF16),
            pltpu.VMEM((TIMES, 384, 128), F32),
            pltpu.VMEM((2, 3, 4, 4, 4, 8, 128), F32),
            pltpu.VMEM((3, 4, 4, 4, 8, 128), F32),
            pltpu.VMEM((3, 3, 4, 4, 8, 128), F32),
            pltpu.VMEM((3, 15, 8, 128), F32),
            pltpu.VMEM((3, 4, 4, 8, 128), F32),
            pltpu.VMEM((3, 8, 128), F32),
            pltpu.VMEM((2, 8, 3, 8, 128), F32),
            pltpu.SemaphoreType.DMA((6,)),
            pltpu.SemaphoreType.DMA((24,)),
            pltpu.SemaphoreType.DMA((24,)),
            pltpu.SemaphoreType.DMA((7,)),
            pltpu.SemaphoreType.DMA((7,)),
            pltpu.SemaphoreType.DMA((6,)),
            pltpu.SemaphoreType.DMA((9,)),
            pltpu.SemaphoreType.DMA((9,)),
            pltpu.SemaphoreType.DMA((6,)),
            pltpu.SemaphoreType.DMA((15,)),
            pltpu.SemaphoreType.DMA((15,)),
        ],
        compiler_params=pltpu.CompilerParams(
            collective_id=0, has_side_effects=True, vmem_limit_bytes=60 * 2**20),
    )(occ, virt, pot, occ_energy[None, :], virt_energy[None, :], times, weights.T)


def solution(mesh):
    return jax.shard_map(
        body,
        mesh=mesh,
        in_specs=(P("pts", None), P("pts", None), P("pts", None), P(), P(), P("tau"), P(None, "tau")),
        out_specs=P("tau", None, None),
        check_vma=False,
    )
```
